32 devices in a mesh: group: 2 (over y), fsdp: 4 (over z), tensor: 2 (over x), seq: 2 (over core).
Axes of the slice: x: 2, y: 2, z: 4, core: 2. Of those that a mesh axis runs over, the one named last changes fastest.
Arguments:
- tokens: bfloat16 [4096, 4096], P(('group', 'fsdp', 'seq'), 'tensor'), parts along dimension 0, may hold values from -6 to 6
- hidden_grad: bfloat16 [4096, 28672], P(('group', 'fsdp', 'seq'), 'tensor'), parts along dimension 0, may hold values from -0.59765625 to 0.59765625
- tile_blocks: bfloat16 [4, 2, 2, 2, 128, 128], P('fsdp', 'tensor'), may hold values from -0.5 to 0.5
- tile_keep: int32 [4, 2, 2, 2], P('fsdp', 'tensor'), may hold values from 0 to 3583, as said below
- tile_count: int32 [4, 2, 2], P('fsdp', 'tensor'), may hold values from 0 to 2, as said below
Outputs:
- token_grad: bfloat16 [4096, 4096], P(('group', 'fsdp', 'seq')), parts along dimension 0
- tile_grads: bfloat16 [8, 2, 2, 2, 128, 128], P(('group', 'fsdp'), 'tensor', 'seq'), parts along dimension 0
The draws below stay inside these ranges and needn't reach their ends.
There are 2 independent parts, one for each index of `group`. The reference program is written for one: setup_inputs(seed, part) draws one part's arguments, and reference() takes and returns one part's arrays. A program takes and returns all parts, laid end to end along the dimension named above; an argument that names none is the same for every part. Nothing has to cross between parts.
Inputs may be any that keep to these rules, and one draw needn't show every extreme that they name: `tile_keep`: within one tensor index and one matrix the live slots of all fsdp shards name distinct blocks; other slots hold arbitrary block numbers. `tile_count`: for every tensor index and matrix the counts over the fsdp shards sum to exactly 4; in each, some shard holds 2 and some holds none.
All inputs are finite; a program needn't handle non-finite values.
Results may differ from the reference program's by a relative error of at most 0.0049.
Values may be sent and summed in bfloat16 or wider, within the bound.
No kernel may reach another device: no remote copies, remote signals or barrier semaphores. Data moves between devices by JAX's collectives and lax.ppermute only.
A program may use at most 192 MiB of HBM per device.

```python
import jax
import jax.numpy as jnp
from jax import lax

D = 4096
FF = 28672
BLK = 128
CAP = 2
SHARDS = 4
SPLITS = 2
NR = 32
NC = 112
LIVE = 4
TOKENS = 2048
N_FSDP = 4
N_TENSOR = 2


def slot_plan(key):
    row_blocks = D // BLK
    col_blocks = FF // (BLK * N_TENSOR)
    block_total = row_blocks * col_blocks
    unit_total = N_FSDP * CAP
    live_total = N_FSDP * CAP // 2

    def one_list(subkey):
        keys = jax.random.split(subkey, 6)
        full_shard = jax.random.randint(keys[0], (), 0, N_FSDP)
        empty_shard = (full_shard + 1 + jax.random.randint(keys[1], (), 0, N_FSDP - 1)) % N_FSDP
        owner = jnp.arange(unit_total, dtype=jnp.int32) // CAP
        priority = jax.random.permutation(keys[2], unit_total).astype(jnp.int32)
        priority = priority + jnp.where(owner == full_shard, unit_total, 0) - jnp.where(owner == empty_shard, 2 * unit_total, 0)
        ordering = jnp.argsort(-priority, stable=True)
        chosen = jnp.zeros((unit_total,), jnp.int32).at[ordering[:live_total]].set(1)
        counts = chosen.reshape(N_FSDP, CAP).sum(axis=1).astype(jnp.int32)
        middle = jax.random.permutation(keys[3], block_total - 2).astype(jnp.int32) + 1
        picked = jnp.concatenate([middle[:live_total - 2], jnp.array([0, block_total - 1], jnp.int32)])
        picked = jax.random.permutation(keys[4], picked)
        offsets = jnp.cumsum(counts).astype(jnp.int32) - counts
        slot_ids = jnp.arange(CAP, dtype=jnp.int32)[None, :]
        live_bool = slot_ids < counts[:, None]
        position = jnp.clip(offsets[:, None] + slot_ids, 0, live_total - 1)
        filler = jax.random.randint(keys[5], (N_FSDP, CAP), 0, block_total)
        blocks = jnp.where(live_bool, picked[position], filler).astype(jnp.int32)
        return (counts, blocks)
    subkeys = jax.random.split(key, N_TENSOR * 2)
    counts, blocks = jax.vmap(one_list)(subkeys)
    counts = counts.reshape(N_TENSOR, 2, N_FSDP).transpose(2, 0, 1)
    blocks = blocks.reshape(N_TENSOR, 2, N_FSDP, CAP).transpose(2, 0, 3, 1)
    return (counts, blocks)


def draw_tile_keep(key, part):
    counts, blocks = slot_plan(key)
    return blocks


def draw_tile_count(key, part):
    counts, blocks = slot_plan(key)
    return counts


def steps_of(rng, extent, pieces, low, high):
    factor_of = 1.0
    for dim, blocks in pieces:
        steps = jax.random.uniform(jax.random.fold_in(jax.random.fold_in(rng, 6), dim), (blocks,), jnp.float32, low / len(pieces), high / len(pieces))
        factor_of = factor_of * jnp.repeat(jnp.exp(steps), extent[dim] // blocks).reshape((-1,) + (1,) * (len(extent) - 1 - dim))
    return factor_of


def normal_values(stream_key, shape, deviation, reach, cuts=(), kind=jnp.bfloat16):
    result = deviation * jax.random.normal(stream_key, shape, jnp.float32)
    if cuts:
        result = result * steps_of(stream_key, shape, cuts, -0.22, 0.18)
    return jnp.clip(result, -reach, reach).astype(kind)


def setup_inputs(seed: int = 0, part: int = 0) -> dict:
    key_of = jax.random.split(jax.random.key(seed), 6)
    part_keys = jax.random.split(jax.random.fold_in(key_of[5], part), 6)
    return {
        "tokens": normal_values(part_keys[0], (TOKENS, D), 1.0, 6.0, ((0, 8), (1, 2))),
        "hidden_grad": normal_values(part_keys[1], (TOKENS, FF), 0.1, 0.59765625, ((0, 8), (1, 2))),
        "tile_blocks": normal_values(key_of[2], (SHARDS, SPLITS, CAP, 2, BLK, BLK), BLK ** -0.5, 0.5, ((0, 4), (1, 2))),
        "tile_keep": draw_tile_keep(jax.random.fold_in(key_of[5], 71), part),
        "tile_count": draw_tile_count(jax.random.fold_in(key_of[5], 71), part),
    }


HIGHEST = lax.Precision.HIGHEST


def slot_terms(x_full, hidden_part, tile_data, row_index, col_index, live_mask):
    tok_rows = x_full.shape[0]
    x_taken = jnp.take(x_full.reshape(tok_rows, NR, BLK), row_index, axis=1).astype(jnp.float32)
    products = jnp.einsum("tsmk,smkn->tsmn", x_taken, tile_data.astype(jnp.float32), precision=HIGHEST)
    col_table = (col_index[:, :, None] == jnp.arange(NC, dtype=jnp.int32)[None, None, :]).astype(jnp.float32) * live_mask[:, :, None]
    pre_acts = jnp.einsum("tsmn,smc->tmcn", products, col_table, precision=HIGHEST)
    gate_pre = pre_acts[:, 0]
    up_pre = pre_acts[:, 1]
    upstream = hidden_part.reshape(tok_rows, NC, BLK).astype(jnp.float32)
    sigmoid_gate = 1.0 / (1.0 + jnp.exp(-gate_pre))
    grad_gate = upstream * up_pre * sigmoid_gate * (1.0 + gate_pre * (1.0 - sigmoid_gate))
    grad_up = upstream * gate_pre * sigmoid_gate
    grad_pair = jnp.stack([grad_gate, grad_up], axis=1).astype(jnp.bfloat16)
    grad_pair = lax.optimization_barrier(grad_pair)
    flat_index = col_index + jnp.arange(2, dtype=jnp.int32)[None, :] * NC
    grad_taken = jnp.take(grad_pair.reshape(tok_rows, 2 * NC, BLK), flat_index, axis=1).astype(jnp.float32)
    back_terms = jnp.einsum("tsmn,smkn->tsmk", grad_taken, tile_data.astype(jnp.float32), precision=HIGHEST)
    row_table = (row_index[:, :, None] == jnp.arange(NR, dtype=jnp.int32)[None, None, :]).astype(jnp.float32) * live_mask[:, :, None]
    token_part = jnp.einsum("tsmk,smr->trk", back_terms, row_table, precision=HIGHEST).reshape(tok_rows, D)
    return x_taken, grad_taken, token_part


def reference(tokens, hidden_grad, tile_blocks, tile_keep, tile_count):
    hidden_width = FF // SPLITS
    slot_total = SHARDS * CAP

    def per_split(carry, split):
        tile_data = lax.dynamic_index_in_dim(tile_blocks, split, 1, keepdims=False).reshape(slot_total, 2, BLK, BLK)
        block_index = lax.dynamic_index_in_dim(tile_keep, split, 1, keepdims=False).reshape(slot_total, 2).astype(jnp.int32)
        counts_here = lax.dynamic_index_in_dim(tile_count, split, 1, keepdims=False).astype(jnp.int32)
        live_bool = (jnp.arange(CAP, dtype=jnp.int32)[None, :, None] < counts_here[:, None, :]).reshape(slot_total, 2)
        picked = jnp.stack([jnp.nonzero(live_bool[:, 0], size=LIVE)[0], jnp.nonzero(live_bool[:, 1], size=LIVE)[0]], axis=1).astype(jnp.int32)
        packed_data = jnp.take_along_axis(tile_data, picked[:, :, None, None], axis=0)
        row_index = jnp.take_along_axis(block_index // NC, picked, axis=0)
        col_index = jnp.take_along_axis(block_index % NC, picked, axis=0)
        hidden_part = lax.dynamic_slice_in_dim(hidden_grad, (split * hidden_width).astype(jnp.int32), hidden_width, 1)
        x_taken, grad_taken, token_part = slot_terms(tokens, hidden_part, packed_data, row_index, col_index, jnp.ones((LIVE, 2), jnp.float32))
        block_grads = jnp.einsum("tsmk,tsmn->smkn", x_taken, grad_taken, precision=HIGHEST)
        slot_rank = jnp.maximum(jnp.cumsum(live_bool.astype(jnp.int32), axis=0).astype(jnp.int32) - 1, 0)
        padded = jnp.take_along_axis(block_grads, slot_rank[:, :, None, None], axis=0) * live_bool.astype(jnp.float32)[:, :, None, None]
        return carry + token_part, padded

    token_sum, split_grads = lax.scan(per_split, jnp.zeros((TOKENS, D), jnp.float32), jnp.arange(SPLITS, dtype=jnp.int32))
    tile_grads = split_grads.reshape(SPLITS, SHARDS, CAP, 2, BLK, BLK).transpose(1, 0, 2, 3, 4, 5).astype(jnp.bfloat16)
    return token_sum.astype(jnp.bfloat16), tile_grads
```

```python
import functools

import jax
import jax.numpy as jnp
from jax import lax
from jax.experimental import pallas as pl
from jax.experimental.pallas import tpu as pltpu
from jax.sharding import PartitionSpec as P

F32 = jnp.float32
BF16 = jnp.bfloat16
VMEM_BYTES = 56 * 2**20


def shift(axis, size, k):
    return [(i, (i + k) % size) for i in range(size)]


def loop(count, body):
    if count <= 8:
        for i in range(count):
            body(i)
    else:
        lax.fori_loop(0, count, lambda i, c: (body(i), c)[1], 0)


def compact(info, row, col, slot, cols):
    shards, width = info.shape
    cap = width // 2
    live = shards * cap // 2
    for m in range(2):
        p = jnp.int32(m * live)
        for k in range(shards):
            for j in range(cap):
                v = info[k, 2 * j + m]
                r = lax.div(v, jnp.int32(cols))
                row[p] = r
                if col is not None:
                    col[p] = v - r * cols
                    slot[p] = k * cap + j
                p = p + jnp.where(v >= 0, 1, 0).astype(jnp.int32)


def find_first(values, first, count):
    def one(i):
        v = values[i]

        def step(n, best):
            at = i - 1 - n
            return jnp.where(values[at] == v, at, best).astype(jnp.int32)

        if isinstance(i, int):
            best = jnp.int32(i)
            for n in range(i):
                best = step(n, best)
        else:
            best = lax.fori_loop(0, i, step, i)
        first[i] = best

    loop(count, one)


def dot(a, b, dims):
    return lax.dot_general(a, b, (dims, ((), ())), preferred_element_type=F32)


def tile_kernel(n_tensor, cols, info, *refs):
    xs, refs = refs[:n_tensor], refs[n_tensor:]
    hid, tiles, back, own, send = refs[:5]
    row, col, slot, cfirst, rfirst, xb, hb, pre, acc, tg, xsem, hsem = refs[5:]
    blk = tiles.shape[-1]
    live = row.shape[0] // 2
    count = 2 * live
    rows_here = xs[0].shape[1] // blk
    t = lax.axis_index("tensor")
    s = lax.axis_index("seq")
    compact(info, row, col, slot, cols)

    def copies(i):
        at = pl.multiple_of(lax.rem(row[i], rows_here) * blk, blk)
        ch = pl.multiple_of(col[i] * blk, blk)
        found = [
            pltpu.make_async_copy(x.at[:, pl.ds(at, blk)], xb.at[n, i], xsem.at[n, i])
            for n, x in enumerate(xs)
        ]
        return found + [pltpu.make_async_copy(hid.at[:, pl.ds(ch, blk)], hb.at[i], hsem.at[i])]

    def start(i):
        for c in copies(i):
            c.start()

    loop(count, start)
    find_first(col, cfirst, count)
    find_first(row, rfirst, count)
    pre[...] = jnp.zeros_like(pre)
    acc[...] = jnp.zeros_like(acc)
    tg[...] = jnp.zeros_like(tg)

    def x_of(i):
        part = lax.rem(lax.div(row[i], rows_here) - t + n_tensor, n_tensor)
        return xb[part, i]

    def forward(i):
        m = i // live
        for c in copies(i):
            c.wait()
        f = cfirst[i]
        pre[m, f] += dot(x_of(i), tiles[2 * slot[i] + m], ((1,), (0,)))

    loop(count, forward)

    def backward(i):
        m = i // live
        f = cfirst[i]
        gate = pre[0, f]
        h = hb[i].astype(F32)
        sig = 1.0 / (1.0 + jnp.exp(-gate))

        def of_gate():
            return h * pre[1, f] * sig * (1.0 + gate * (1.0 - sig))

        def of_up():
            return h * gate * sig

        if isinstance(m, int):
            grad = of_up() if m else of_gate()
        else:
            grad = jnp.where(m == 0, of_gate(), of_up())
        grad = grad.astype(BF16)
        w = tiles[2 * slot[i] + m]
        acc[rfirst[i]] += dot(grad, w, ((1,), (1,)))
        at = slot[i]
        tg[lax.rem(at, 2), lax.div(at, 2), m] = dot(x_of(i), grad, ((0,), (0,)))

    loop(count, backward)
    back[...] = acc[...].astype(BF16)
    own[...] = tg[s]
    send[...] = tg[1 - s]


def final_kernel(n_tensor, shards, cols, infos, *refs):
    parts, refs = refs[:n_tensor], refs[n_tensor:]
    mine, refs = refs[0], refs[1:]
    others, refs = refs[: shards - 1], refs[shards - 1 :]
    token_grad, tile_grads, row, wide = refs
    count, _, blk = parts[0].shape
    total = token_grad if n_tensor == 2 else wide
    total[...] = jnp.zeros_like(total)
    for n in range(n_tensor):
        compact(infos.at[n], row, None, None, cols)

        def add(i):
            at = pl.ds(pl.multiple_of(row[i] * blk, blk), blk)
            total[:, at] = (total[:, at].astype(F32) + parts[n][i].astype(F32)).astype(total.dtype)

        loop(count, add)
    if n_tensor != 2:
        token_grad[...] = wide[...].astype(BF16)
    tile_sum = mine[...]
    for other in others:
        tile_sum = tile_sum + other[...].astype(F32)
    tile_grads[...] = tile_sum.astype(BF16)


def local(sizes, tokens, hidden_grad, tile_blocks, tile_keep, tile_count):
    shards, n_tensor = sizes["fsdp"], sizes["tensor"]
    blk = tile_blocks.shape[-1]
    cap = tile_blocks.shape[2]
    toks = tokens.shape[0]
    width = tokens.shape[1] * n_tensor
    cols = hidden_grad.shape[1] // blk
    live = shards * cap // 2
    count = 2 * live
    vmem = pl.BlockSpec(memory_space=pltpu.VMEM)
    smem = pl.BlockSpec(memory_space=pltpu.SMEM)
    hbm = pl.BlockSpec(memory_space=pl.ANY)
    params = pltpu.CompilerParams(vmem_limit_bytes=VMEM_BYTES)

    is_live = jnp.arange(cap, dtype=jnp.int32)[None, :, None] < tile_count.reshape(1, 1, 2)
    info = jnp.where(is_live, tile_keep.reshape(1, cap, 2), -1).reshape(1, 2 * cap)
    tiles = tile_blocks.reshape(2 * cap, blk, blk)

    def from_shards(a):
        return [a] + [lax.ppermute(a, "fsdp", shift("fsdp", shards, k)) for k in range(1, shards)]

    xs = [tokens] + [
        lax.ppermute(tokens, "tensor", shift("tensor", n_tensor, n_tensor - k))
        for k in range(1, n_tensor)
    ]
    info_all = jnp.concatenate(from_shards(info), axis=0)
    tiles_all = jnp.concatenate(from_shards(tiles), axis=0)

    back, own, send = pl.pallas_call(
        functools.partial(tile_kernel, n_tensor, cols),
        out_shape=(
            jax.ShapeDtypeStruct((count, toks, blk), BF16),
            jax.ShapeDtypeStruct((shards, 2, blk, blk), F32),
            jax.ShapeDtypeStruct((shards, 2, blk, blk), F32),
        ),
        in_specs=[smem] + [hbm] * n_tensor + [hbm, vmem],
        out_specs=(vmem, vmem, vmem),
        scratch_shapes=[
            pltpu.SMEM((count + 1,), jnp.int32),
            pltpu.SMEM((count + 1,), jnp.int32),
            pltpu.SMEM((count + 1,), jnp.int32),
            pltpu.SMEM((count,), jnp.int32),
            pltpu.SMEM((count,), jnp.int32),
            pltpu.VMEM((n_tensor, count, toks, blk), BF16),
            pltpu.VMEM((count, toks, blk), BF16),
            pltpu.VMEM((2, count, toks, blk), F32),
            pltpu.VMEM((count, toks, blk), F32),
            pltpu.VMEM((cap, shards, 2, blk, blk), F32),
            pltpu.SemaphoreType.DMA((n_tensor, count)),
            pltpu.SemaphoreType.DMA((count,)),
        ],
        compiler_params=params,
        name="tile_terms",
    )(info_all, *xs, hidden_grad, tiles_all)

    if n_tensor == 2:
        swap = shift("tensor", 2, 1)
        parts = [back, lax.ppermute(back, "tensor", swap)]
        infos = jnp.stack([info_all, lax.ppermute(info_all, "tensor", swap)])
    else:
        gathered = lax.all_gather(back, "tensor")
        parts = [gathered[n] for n in range(n_tensor)]
        infos = lax.all_gather(info_all, "tensor")

    pair = own + lax.ppermute(send, "seq", shift("seq", 2, 1))
    rounded = pair.astype(BF16)
    others = [
        lax.ppermute(rounded[k], "fsdp", shift("fsdp", shards, shards - k)) for k in range(1, shards)
    ]

    token_grad, tile_grads = pl.pallas_call(
        functools.partial(final_kernel, n_tensor, shards, cols),
        out_shape=(
            jax.ShapeDtypeStruct((toks, width), BF16),
            jax.ShapeDtypeStruct((2, blk, blk), BF16),
        ),
        in_specs=[smem] + [vmem] * (n_tensor + shards),
        out_specs=(vmem, vmem),
        scratch_shapes=[
            pltpu.SMEM((count + 1,), jnp.int32),
            pltpu.VMEM((toks, width) if n_tensor != 2 else (8, 128), F32),
        ],
        compiler_params=params,
        name="assemble",
    )(infos, *parts, pair[0], *others)
    return token_grad, tile_grads.reshape(1, 1, 1, 2, blk, blk)


def solution(mesh):
    return jax.shard_map(
        functools.partial(local, dict(mesh.shape)),
        mesh=mesh,
        in_specs=(
            P(("group", "fsdp", "seq"), "tensor"),
            P(("group", "fsdp", "seq"), "tensor"),
            P("fsdp", "tensor", None, None, None, None),
            P("fsdp", "tensor", None, None),
            P("fsdp", "tensor", None),
        ),
        out_specs=(
            P(("group", "fsdp", "seq"), None),
            P(("group", "fsdp"), "tensor", "seq", None, None, None),
        ),
        check_vma=False,
    )
```

```python
import functools

import jax
import jax.numpy as jnp
from jax import lax
from jax.experimental import pallas as pl
from jax.experimental.pallas import tpu as pltpu
from jax.sharding import PartitionSpec as P

F32 = jnp.float32
BF16 = jnp.bfloat16
I32 = jnp.int32
ROW, COL, SLOT, CFIRST, RFIRST = range(5)
INFO_ROWS = 16


def shift(size, k):
    return [(i, (i + k) % size) for i in range(size)]


def swaps(size, k):
    return [(i, i ^ k) for i in range(size)]


def loop(count, body):
    if count <= 8:
        for i in range(count):
            body(i)
    else:
        lax.fori_loop(0, count, lambda i, c: (body(i), c)[1], 0)


def find_first(table, src, dst, count):
    def one(i):
        v = table[src, i]

        def step(n, best):
            at = i - 1 - n
            return jnp.where(table[src, at] == v, at, best).astype(I32)

        if isinstance(i, int):
            best = jnp.int32(i)
            for n in range(i):
                best = step(n, best)
        else:
            best = lax.fori_loop(0, i, step, i)
        table[dst, i] = best

    loop(count, one)


def cost(us):
    return pl.CostEstimate(flops=0, bytes_accessed=int(us * 3.69e6), transcendentals=0)


def dot(a, b, dims):
    return lax.dot_general(a, b, (dims, ((), ())), preferred_element_type=F32)


def pack_kernel(cols, keep, count, tiles, packed):
    _, _, cap, _, blk, _ = tiles.shape
    for j in range(cap):
        for m in range(2):
            packed[pl.ds((2 * j + m) * blk, blk), :] = tiles[0, 0, j, m]
    line = lax.broadcasted_iota(I32, (INFO_ROWS, blk), 0)
    lane = lax.broadcasted_iota(I32, (INFO_ROWS, blk), 1)
    info = jnp.zeros((INFO_ROWS, blk), I32)
    for j in range(cap):
        for m in range(2):
            b = keep[0, 0, j, m]
            r = lax.div(b, jnp.int32(cols))
            c = b - r * cols
            r = jnp.where(j < count[0, 0, m], r, -1)
            here = lane == 2 * j + m
            info = jnp.where(here & (line == 0), r, jnp.where(here & (line == 1), c, info))
    packed[pl.ds(2 * cap * blk, INFO_ROWS), :] = info.astype(F32).astype(BF16)


def prepare_kernel(shards, cap, *refs):
    packed, refs = refs[:shards], refs[shards:]
    tokens, hidden, table, weights, xo, hb, ints, info, isem, xsem, hsem = refs
    blk = weights.shape[-1]
    base = 2 * cap * blk
    rows_here = tokens.shape[1] // blk
    count = xo.shape[0]
    live = count // 2
    for k in range(shards):
        ints[k] = packed[k][pl.ds(base, INFO_ROWS), :].astype(F32)[:8].astype(I32)
    fetch = pltpu.make_async_copy(ints, info, isem)
    fetch.start()
    fetch.wait()
    for m in range(2):
        p = jnp.int32(m * live)
        for k in range(shards):
            for j in range(cap):
                r = info[k, 0, 2 * j + m]
                table[ROW, p] = r
                table[COL, p] = info[k, 1, 2 * j + m]
                table[SLOT, p] = k * cap + j
                weights[p] = packed[k][pl.ds((2 * j + m) * blk, blk), :]
                p = p + jnp.where(r >= 0, 1, 0).astype(I32)

    def copies(i):
        at = pl.multiple_of(lax.rem(table[ROW, i], rows_here) * blk, blk)
        ch = pl.multiple_of(table[COL, i] * blk, blk)
        return (
            pltpu.make_async_copy(tokens.at[:, pl.ds(at, blk)], xo.at[i], xsem.at[i]),
            pltpu.make_async_copy(hidden.at[:, pl.ds(ch, blk)], hb.at[i], hsem.at[i]),
        )

    def start(i):
        for c in copies(i):
            c.start()

    def wait(i):
        for c in copies(i):
            c.wait()

    loop(count, start)
    find_first(table, COL, CFIRST, count)
    find_first(table, ROW, RFIRST, count)
    loop(count, wait)


def forward_backward(lo, table, weights, xo, hb, remote, xs, pre, grads):
    count, size, blk = xs.shape
    live = count // 2
    rows_here = remote[0].shape[1] // blk
    n_tensor = len(remote) + 1
    t = lax.axis_index("tensor")
    pre[...] = jnp.zeros_like(pre)

    def forward(i):
        r = table[ROW, i]
        part = lax.rem(lax.div(r, rows_here) - t + n_tensor, n_tensor)
        at = pl.multiple_of(lax.rem(r, rows_here) * blk, blk)
        x = xo[i, pl.ds(lo, size), :]
        for n, ref in enumerate(remote):
            x = jnp.where(part == n + 1, ref[:, pl.ds(at, blk)], x)
        xs[i] = x
        pre[i // live, table[CFIRST, i]] += dot(x, weights[i], ((1,), (0,)))

    loop(count, forward)

    def backward(i):
        m = i // live
        f = table[CFIRST, i]
        gate = pre[0, f]
        h = hb[i, pl.ds(lo, size), :].astype(F32)
        sig = 1.0 / (1.0 + jnp.exp(-gate))

        def of_gate():
            return h * pre[1, f] * sig * (1.0 + gate * (1.0 - sig))

        def of_up():
            return h * gate * sig

        if isinstance(m, int):
            grad = of_up() if m else of_gate()
        else:
            grad = jnp.where(m == 0, of_gate(), of_up())
        grads[i] = grad.astype(BF16)

    loop(count, backward)


def back_terms(table, weights, grads, acc, back):
    count, size, _ = acc.shape
    acc[...] = jnp.zeros_like(acc)

    def one(i):
        acc[table[RFIRST, i]] += dot(grads[i], weights[i], ((1,), (1,)))

    def put(i):
        back[pl.ds(pl.multiple_of(i * size, size), size), :] = acc[i].astype(BF16)

    loop(count, one)
    loop(count, put)


def first_kernel(n_tensor, table, weights, xo, hb, *refs):
    remote, refs = refs[: n_tensor - 1], refs[n_tensor - 1 :]
    back, tile_sums, xs, pre, grads, acc = refs
    forward_backward(0, table, weights, xo, hb, remote, xs, pre, grads)

    def tile(i):
        tile_sums[i] = dot(xs[i], grads[i], ((0,), (0,)))

    count, size, blk = xs.shape
    loop(count, tile)
    back_terms(table, weights, grads, acc, back)
    lane = lax.broadcasted_iota(I32, (INFO_ROWS, blk), 1)
    rows = jnp.zeros((INFO_ROWS, blk), I32)
    for i in range(count):
        rows = jnp.where(lane == i, table[ROW, i], rows)
    back[pl.ds(count * size, INFO_ROWS), :] = rows.astype(F32).astype(BF16)


def second_kernel(n_tensor, lo, cap, table, weights, xo, hb, tile_sums, *refs):
    remote, refs = refs[: n_tensor - 1], refs[n_tensor - 1 :]
    own, send, grads, xs, pre, both = refs
    forward_backward(lo, table, weights, xo, hb, remote, xs, pre, grads)
    both[...] = jnp.zeros_like(both)
    s = lax.axis_index("seq")
    live = xs.shape[0] // 2

    def tile(i):
        value = tile_sums[i] + dot(xs[i], grads[i], ((0,), (0,)))
        slot = table[SLOT, i]
        both[lax.rem(slot + s, cap), lax.div(slot, cap), i // live] = value

    loop(xs.shape[0], tile)
    own[...] = both[0]
    send[...] = both[1].astype(send.dtype)


def back_kernel(table, weights, grads, back, acc):
    back_terms(table, weights, grads, acc, back)


def add_blocks(rows, parts, count, block, wide, out, lo, sem):
    size = block.shape[0]
    blk = parts[0].shape[1]
    n_tensor = len(parts)
    total = block if n_tensor == 2 else wide
    total[...] = jnp.zeros_like(total)
    for n, part in enumerate(parts):

        def add(i):
            at = pl.ds(pl.multiple_of(rows[n, i] * blk, blk), blk)
            term = part[pl.ds(pl.multiple_of(i * size, size), size), :].astype(F32)
            total[:, at] = (total[:, at].astype(F32) + term).astype(total.dtype)

        loop(count, add)
    if n_tensor != 2:
        block[...] = wide[...].astype(BF16)
    copy = pltpu.make_async_copy(block, out.at[pl.ds(lo, size), :], sem)
    copy.start()
    return copy


def place_early_kernel(n_tensor, count, *refs):
    parts, refs = refs[:n_tensor], refs[n_tensor:]
    out, rows, ints, info, block, wide, isem, sem = refs
    size = block.shape[0]
    for n, part in enumerate(parts):
        ints[n] = part[pl.ds(count * size, INFO_ROWS), :].astype(F32)[:8].astype(I32)
    fetch = pltpu.make_async_copy(ints, info, isem)
    fetch.start()
    fetch.wait()
    for n in range(n_tensor):
        for i in range(count):
            rows[n, i] = info[n, 0, i]
    add_blocks(rows, parts, count, block, wide, out, 0, sem).wait()


def place_late_kernel(n_tensor, lo, count, rows, *refs):
    parts, refs = refs[:n_tensor], refs[n_tensor:]
    _, mine, *others, out, tile_grads, block, wide, sem = refs
    copy = add_blocks(rows, parts, count, block, wide, out, lo, sem)
    tile_sum = mine[...]
    for other in others:
        tile_sum = tile_sum + other[...].astype(F32)
    tile_grads[...] = tile_sum.astype(BF16)
    copy.wait()


def local(sizes, tokens, hidden_grad, tile_blocks, tile_keep, tile_count):
    shards, n_tensor = sizes["fsdp"], sizes["tensor"]
    blk = tile_blocks.shape[-1]
    cap = tile_blocks.shape[2]
    toks = tokens.shape[0]
    width = tokens.shape[1] * n_tensor
    cols = hidden_grad.shape[1] // blk
    count = shards * cap
    cut = toks * 3 // 4 // 16 * 16
    rest = toks - cut
    vmem = pl.BlockSpec(memory_space=pltpu.VMEM)
    smem = pl.BlockSpec(memory_space=pltpu.SMEM)
    hbm = pl.BlockSpec(memory_space=pltpu.HBM)
    spare = pltpu.CompilerParams(vmem_limit_bytes=(16 if count <= 8 else 40) * 2**20)
    swap = shift(2, 1)

    def shape(dims, kind):
        return jax.ShapeDtypeStruct(dims, kind)

    def to_partners(a):
        return [
            lax.ppermute(a, "tensor", shift(n_tensor, n_tensor - k)) for k in range(1, n_tensor)
        ]

    early = to_partners(tokens[:cut])
    packed = pl.pallas_call(
        functools.partial(pack_kernel, cols),
        out_shape=shape((2 * cap * blk + INFO_ROWS, blk), BF16),
        in_specs=[smem, smem, vmem],
        out_specs=vmem,
        compiler_params=spare,
        cost_estimate=cost(0.001),
        name="pack",
    )(tile_keep, tile_count, tile_blocks)
    late = to_partners(tokens[cut:])
    gathered = [packed] + [
        lax.ppermute(packed, "fsdp", swaps(shards, k)) for k in range(1, shards)
    ]

    table, weights, xo, hb = pl.pallas_call(
        functools.partial(prepare_kernel, shards, cap),
        out_shape=(
            shape((5, count + 1), I32),
            shape((count + 1, blk, blk), BF16),
            shape((count, toks, blk), BF16),
            shape((count, toks, blk), BF16),
        ),
        in_specs=[vmem] * shards + [hbm, hbm],
        out_specs=(smem, vmem, vmem, vmem),
        scratch_shapes=[
            pltpu.VMEM((shards, 8, blk), I32),
            pltpu.SMEM((shards, 8, blk), I32),
            pltpu.SemaphoreType.DMA,
            pltpu.SemaphoreType.DMA((count,)),
            pltpu.SemaphoreType.DMA((count,)),
        ],
        compiler_params=pltpu.CompilerParams(vmem_limit_bytes=50 * 2**20),
        cost_estimate=cost(0.001),
        name="prepare",
    )(*gathered, tokens, hidden_grad)

    back_early, tile_sums = pl.pallas_call(
        functools.partial(first_kernel, n_tensor),
        out_shape=(shape((count * cut + INFO_ROWS, blk), BF16), shape((count, blk, blk), F32)),
        in_specs=[smem] + [vmem] * (2 + n_tensor),
        out_specs=(vmem, vmem),
        scratch_shapes=[
            pltpu.VMEM((count, cut, blk), BF16),
            pltpu.VMEM((2, count, cut, blk), F32),
            pltpu.VMEM((count, cut, blk), BF16),
            pltpu.VMEM((count, cut, blk), F32),
        ],
        compiler_params=spare,
        cost_estimate=cost(0.001),
        name="early_terms",
    )(table, weights, xo, hb, *early)

    own, send, grads = pl.pallas_call(
        functools.partial(second_kernel, n_tensor, cut, cap),
        out_shape=(
            shape((shards, 2, blk, blk), F32),
            shape((shards, 2, blk, blk), F32),
            shape((count, rest, blk), BF16),
        ),
        in_specs=[smem] + [vmem] * (3 + n_tensor),
        out_specs=(vmem,) * 3,
        scratch_shapes=[
            pltpu.VMEM((count, rest, blk), BF16),
            pltpu.VMEM((2, count, rest, blk), F32),
            pltpu.VMEM((cap, shards, 2, blk, blk), F32),
        ],
        compiler_params=spare,
        cost_estimate=cost(0.001),
        name="late_tiles",
    )(table, weights, xo, hb, tile_sums, *late)
    other = lax.ppermute(send, "seq", swap)
    pairs = [own[k] + other[k].astype(F32) for k in range(shards)]
    others = [
        lax.ppermute(pairs[k].astype(BF16), "fsdp", swaps(shards, k)) for k in range(1, shards)
    ]

    back_late = pl.pallas_call(
        back_kernel,
        out_shape=shape((count * rest, blk), BF16),
        in_specs=[smem, vmem, vmem],
        out_specs=vmem,
        scratch_shapes=[pltpu.VMEM((count, rest, blk), F32)],
        compiler_params=spare,
        cost_estimate=cost(0.001),
        name="late_terms",
    )(table, weights, grads)

    def of_all(a):
        if n_tensor == 2:
            return [a, lax.ppermute(a, "tensor", swap)]
        everyone = lax.all_gather(a, "tensor")
        return [everyone[n] for n in range(n_tensor)]

    def block_scratch(size):
        return [
            pltpu.VMEM((size, width), BF16),
            pltpu.VMEM((size, width) if n_tensor != 2 else (8, 128), F32),
        ]

    token_grad, rows = pl.pallas_call(
        functools.partial(place_early_kernel, n_tensor, count),
        out_shape=(shape((toks, width), BF16), shape((n_tensor, count), I32)),
        in_specs=[vmem] * n_tensor,
        out_specs=(hbm, smem),
        scratch_shapes=[
            pltpu.VMEM((n_tensor, 8, blk), I32),
            pltpu.SMEM((n_tensor, 8, blk), I32),
            *block_scratch(cut),
            pltpu.SemaphoreType.DMA,
            pltpu.SemaphoreType.DMA,
        ],
        compiler_params=spare,
        cost_estimate=cost(0.001),
        name="place_early",
    )(*of_all(back_early))
    token_grad, tile_grads = pl.pallas_call(
        functools.partial(place_late_kernel, n_tensor, cut, count),
        out_shape=(shape((toks, width), BF16), shape((2, blk, blk), BF16)),
        in_specs=[smem] + [vmem] * n_tensor + [hbm] + [vmem] * shards,
        out_specs=(hbm, vmem),
        scratch_shapes=[*block_scratch(rest), pltpu.SemaphoreType.DMA],
        input_output_aliases={n_tensor + 1: 0},
        compiler_params=spare,
        cost_estimate=cost(0.001),
        name="place_late",
    )(rows, *of_all(back_late), token_grad, pairs[0], *others)
    return token_grad, tile_grads.reshape(1, 1, 1, 2, blk, blk)


def solution(mesh):
    return jax.shard_map(
        functools.partial(local, dict(mesh.shape)),
        mesh=mesh,
        in_specs=(
            P(("group", "fsdp", "seq"), "tensor"),
            P(("group", "fsdp", "seq"), "tensor"),
            P("fsdp", "tensor", None, None, None, None),
            P("fsdp", "tensor", None, None),
            P("fsdp", "tensor", None),
        ),
        out_specs=(
            P(("group", "fsdp", "seq"), None),
            P(("group", "fsdp"), "tensor", "seq", None, None, None),
        ),
        check_vma=False,
    )
```

```python
import functools

import jax
import jax.numpy as jnp
from jax import lax
from jax.experimental import pallas as pl
from jax.experimental.pallas import tpu as pltpu
from jax.sharding import PartitionSpec as P

F32 = jnp.float32
BF16 = jnp.bfloat16
I32 = jnp.int32
ROW, COL, SLOT, CFIRST, RFIRST = range(5)
INFO_ROWS = 16


def shift(size, k):
    return [(i, (i + k) % size) for i in range(size)]


def swaps(size, k):
    return [(i, i ^ k) for i in range(size)]


def loop(count, body):
    if count <= 8:
        for i in range(count):
            body(i)
    else:
        lax.fori_loop(0, count, lambda i, c: (body(i), c)[1], 0)


def find_first(table, src, dst, count):
    def one(i):
        v = table[src, i]

        def step(n, best):
            at = i - 1 - n
            return jnp.where(table[src, at] == v, at, best).astype(I32)

        if isinstance(i, int):
            best = jnp.int32(i)
            for n in range(i):
                best = step(n, best)
        else:
            best = lax.fori_loop(0, i, step, i)
        table[dst, i] = best

    loop(count, one)


def cost(us):
    return pl.CostEstimate(flops=0, bytes_accessed=int(us * 3.69e6), transcendentals=0)


def dot(a, b, dims):
    return lax.dot_general(a, b, (dims, ((), ())), preferred_element_type=F32)


def pack_kernel(cols, keep, count, tiles, packed):
    _, _, cap, _, blk, _ = tiles.shape
    for j in range(cap):
        for m in range(2):
            packed[pl.ds((2 * j + m) * blk, blk), :] = tiles[0, 0, j, m]
    line = lax.broadcasted_iota(I32, (INFO_ROWS, blk), 0)
    lane = lax.broadcasted_iota(I32, (INFO_ROWS, blk), 1)
    info = jnp.zeros((INFO_ROWS, blk), I32)
    for j in range(cap):
        for m in range(2):
            b = keep[0, 0, j, m]
            r = lax.div(b, jnp.int32(cols))
            c = b - r * cols
            r = jnp.where(j < count[0, 0, m], r, -1)
            here = lane == 2 * j + m
            info = jnp.where(here & (line == 0), r, jnp.where(here & (line == 1), c, info))
    packed[pl.ds(2 * cap * blk, INFO_ROWS), :] = info.astype(F32).astype(BF16)


def prepare_kernel(shards, cap, *refs):
    packed, refs = refs[:shards], refs[shards:]
    tokens, hidden, table, weights, xo, hb, ints, info, isem, xsem, hsem = refs
    blk = weights.shape[-1]
    base = 2 * cap * blk
    rows_here = tokens.shape[1] // blk
    count = xo.shape[0]
    live = count // 2
    for k in range(shards):
        ints[k] = packed[k][pl.ds(base, INFO_ROWS), :].astype(F32)[:8].astype(I32)
    fetch = pltpu.make_async_copy(ints, info, isem)
    fetch.start()
    fetch.wait()
    for m in range(2):
        p = jnp.int32(m * live)
        for k in range(shards):
            for j in range(cap):
                r = info[k, 0, 2 * j + m]
                table[ROW, p] = r
                table[COL, p] = info[k, 1, 2 * j + m]
                table[SLOT, p] = k * cap + j
                weights[p] = packed[k][pl.ds((2 * j + m) * blk, blk), :]
                p = p + jnp.where(r >= 0, 1, 0).astype(I32)

    def copies(i):
        at = pl.multiple_of(lax.rem(table[ROW, i], rows_here) * blk, blk)
        ch = pl.multiple_of(table[COL, i] * blk, blk)
        return (
            pltpu.make_async_copy(tokens.at[:, pl.ds(at, blk)], xo.at[i], xsem.at[i]),
            pltpu.make_async_copy(hidden.at[:, pl.ds(ch, blk)], hb.at[i], hsem.at[i]),
        )

    def start(i):
        for c in copies(i):
            c.start()

    def wait(i):
        for c in copies(i):
            c.wait()

    loop(count, start)
    find_first(table, COL, CFIRST, count)
    find_first(table, ROW, RFIRST, count)
    loop(count, wait)


def forward_backward(lo, table, weights, xo, hb, remote, xs, pre, grads):
    count, size, blk = xs.shape
    live = count // 2
    rows_here = remote[0].shape[1] // blk
    n_tensor = len(remote) + 1
    t = lax.axis_index("tensor")
    pre[...] = jnp.zeros_like(pre)

    def forward(i):
        r = table[ROW, i]
        part = lax.rem(lax.div(r, rows_here) - t + n_tensor, n_tensor)
        at = pl.multiple_of(lax.rem(r, rows_here) * blk, blk)
        x = xo[i, pl.ds(lo, size), :]
        for n, ref in enumerate(remote):
            x = jnp.where(part == n + 1, ref[:, pl.ds(at, blk)], x)
        xs[i] = x
        pre[i // live, table[CFIRST, i]] += dot(x, weights[i], ((1,), (0,)))

    loop(count, forward)

    def backward(i):
        m = i // live
        f = table[CFIRST, i]
        gate = pre[0, f]
        h = hb[i, pl.ds(lo, size), :].astype(F32)
        sig = 1.0 / (1.0 + jnp.exp(-gate))

        def of_gate():
            return h * pre[1, f] * sig * (1.0 + gate * (1.0 - sig))

        def of_up():
            return h * gate * sig

        if isinstance(m, int):
            grad = of_up() if m else of_gate()
        else:
            grad = jnp.where(m == 0, of_gate(), of_up())
        grads[i] = grad.astype(BF16)

    loop(count, backward)


def back_terms(table, weights, grads, acc, back):
    count, size, _ = acc.shape
    acc[...] = jnp.zeros_like(acc)

    def one(i):
        acc[table[RFIRST, i]] += dot(grads[i], weights[i], ((1,), (1,)))

    def put(i):
        back[pl.ds(pl.multiple_of(i * size, size), size), :] = acc[i].astype(BF16)

    loop(count, one)
    loop(count, put)


def first_kernel(n_tensor, table, weights, xo, hb, *refs):
    remote, refs = refs[: n_tensor - 1], refs[n_tensor - 1 :]
    back, tile_sums, xs, pre, grads, acc = refs
    forward_backward(0, table, weights, xo, hb, remote, xs, pre, grads)

    def tile(i):
        tile_sums[i] = dot(xs[i], grads[i], ((0,), (0,)))

    count, size, blk = xs.shape
    loop(count, tile)
    back_terms(table, weights, grads, acc, back)
    lane = lax.broadcasted_iota(I32, (INFO_ROWS, blk), 1)
    rows = jnp.zeros((INFO_ROWS, blk), I32)
    for i in range(count):
        rows = jnp.where(lane == i, table[ROW, i], rows)
    back[pl.ds(count * size, INFO_ROWS), :] = rows.astype(F32).astype(BF16)


def second_kernel(n_tensor, lo, cap, table, weights, xo, hb, tile_sums, *refs):
    remote, refs = refs[: n_tensor - 1], refs[n_tensor - 1 :]
    own, send, back, grads, xs, pre, both, acc = refs
    forward_backward(lo, table, weights, xo, hb, remote, xs, pre, grads)
    both[...] = jnp.zeros_like(both)
    s = lax.axis_index("seq")
    live = xs.shape[0] // 2

    def tile(i):
        value = tile_sums[i] + dot(xs[i], grads[i], ((0,), (0,)))
        slot = table[SLOT, i]
        both[lax.rem(slot + s, cap), lax.div(slot, cap), i // live] = value

    loop(xs.shape[0], tile)
    own[...] = both[0]
    send[...] = both[1].astype(send.dtype)
    back_terms(table, weights, grads, acc, back)


def pair_kernel(own, other, *sums):
    for k, total in enumerate(sums):
        total[...] = (own[k] + other[k].astype(F32)).astype(total.dtype)


def add_blocks(rows, parts, count, block, wide, out, lo, sem):
    size = block.shape[0]
    blk = parts[0].shape[1]
    n_tensor = len(parts)
    total = block if n_tensor == 2 else wide
    total[...] = jnp.zeros_like(total)
    for n, part in enumerate(parts):

        def add(i):
            at = pl.ds(pl.multiple_of(rows[n, i] * blk, blk), blk)
            term = part[pl.ds(pl.multiple_of(i * size, size), size), :].astype(F32)
            total[:, at] = (total[:, at].astype(F32) + term).astype(total.dtype)

        loop(count, add)
    if n_tensor != 2:
        block[...] = wide[...].astype(BF16)
    copy = pltpu.make_async_copy(block, out.at[pl.ds(lo, size), :], sem)
    copy.start()
    return copy


def place_early_kernel(n_tensor, count, *refs):
    infos, refs = refs[:n_tensor], refs[n_tensor:]
    parts, refs = refs[:n_tensor], refs[n_tensor:]
    out, rows, ints, info, isem, block, wide, sem = refs
    for n, part in enumerate(infos):
        ints[n] = part[...].astype(F32)[:8].astype(I32)
    fetch = pltpu.make_async_copy(ints, info, isem)
    fetch.start()
    fetch.wait()
    for n in range(n_tensor):
        for i in range(count):
            rows[n, i] = info[n, 0, i]
    add_blocks(rows, parts, count, block, wide, out, 0, sem).wait()


def place_late_kernel(n_tensor, shards, lo, count, rows, *refs):
    parts, refs = refs[:n_tensor], refs[n_tensor:]
    _, mine, *others = refs[: shards + 1]
    out, tile_grads, block, wide, sem, tile_sum, tile_sem = refs[shards + 1 :]
    total = mine[...]
    for other in others:
        total = total + other[...].astype(F32)
    tile_sum[...] = total.astype(BF16)
    tile_copy = pltpu.make_async_copy(tile_sum, tile_grads, tile_sem)
    tile_copy.start()
    copy = add_blocks(rows, parts, count, block, wide, out, lo, sem)
    tile_copy.wait()
    copy.wait()


def local(sizes, tokens, hidden_grad, tile_blocks, tile_keep, tile_count):
    shards, n_tensor = sizes["fsdp"], sizes["tensor"]
    blk = tile_blocks.shape[-1]
    cap = tile_blocks.shape[2]
    toks = tokens.shape[0]
    width = tokens.shape[1] * n_tensor
    cols = hidden_grad.shape[1] // blk
    count = shards * cap
    cut = toks * 3 // 4 // 16 * 16
    rest = toks - cut
    vmem = pl.BlockSpec(memory_space=pltpu.VMEM)
    smem = pl.BlockSpec(memory_space=pltpu.SMEM)
    hbm = pl.BlockSpec(memory_space=pltpu.HBM)
    spare = pltpu.CompilerParams(vmem_limit_bytes=(16 if count <= 8 else 40) * 2**20)
    swap = shift(2, 1)

    def shape(dims, kind):
        return jax.ShapeDtypeStruct(dims, kind)

    def to_partners(a):
        return [
            lax.ppermute(a, "tensor", shift(n_tensor, n_tensor - k)) for k in range(1, n_tensor)
        ]

    early = to_partners(tokens[:cut])
    packed = pl.pallas_call(
        functools.partial(pack_kernel, cols),
        out_shape=shape((2 * cap * blk + INFO_ROWS, blk), BF16),
        in_specs=[smem, smem, vmem],
        out_specs=vmem,
        compiler_params=spare,
        cost_estimate=cost(0.001),
        name="pack",
    )(tile_keep, tile_count, tile_blocks)
    late = to_partners(tokens[cut:])
    gathered = [packed] + [
        lax.ppermute(packed, "fsdp", swaps(shards, k)) for k in range(1, shards)
    ]

    table, weights, xo, hb = pl.pallas_call(
        functools.partial(prepare_kernel, shards, cap),
        out_shape=(
            shape((5, count + 1), I32),
            shape((count + 1, blk, blk), BF16),
            shape((count, toks, blk), BF16),
            shape((count, toks, blk), BF16),
        ),
        in_specs=[vmem] * shards + [hbm, hbm],
        out_specs=(smem, vmem, vmem, vmem),
        scratch_shapes=[
            pltpu.VMEM((shards, 8, blk), I32),
            pltpu.SMEM((shards, 8, blk), I32),
            pltpu.SemaphoreType.DMA,
            pltpu.SemaphoreType.DMA((count,)),
            pltpu.SemaphoreType.DMA((count,)),
        ],
        compiler_params=pltpu.CompilerParams(vmem_limit_bytes=50 * 2**20),
        cost_estimate=cost(0.001),
        name="prepare",
    )(*gathered, tokens, hidden_grad)

    back_early, tile_sums = pl.pallas_call(
        functools.partial(first_kernel, n_tensor),
        out_shape=(shape((count * cut + INFO_ROWS, blk), BF16), shape((count, blk, blk), F32)),
        in_specs=[smem] + [vmem] * (2 + n_tensor),
        out_specs=(vmem, vmem),
        scratch_shapes=[
            pltpu.VMEM((count, cut, blk), BF16),
            pltpu.VMEM((2, count, cut, blk), F32),
            pltpu.VMEM((count, cut, blk), BF16),
            pltpu.VMEM((count, cut, blk), F32),
        ],
        compiler_params=spare,
        cost_estimate=cost(0.001),
        name="early_terms",
    )(table, weights, xo, hb, *early)

    own, send, back_late = pl.pallas_call(
        functools.partial(second_kernel, n_tensor, cut, cap),
        out_shape=(
            shape((shards, 2, blk, blk), F32),
            shape((shards, 2, blk, blk), BF16),
            shape((count * rest, blk), BF16),
        ),
        in_specs=[smem] + [vmem] * (3 + n_tensor),
        out_specs=(vmem,) * 3,
        scratch_shapes=[
            pltpu.VMEM((count, rest, blk), BF16),
            pltpu.VMEM((count, rest, blk), BF16),
            pltpu.VMEM((2, count, rest, blk), F32),
            pltpu.VMEM((cap, shards, 2, blk, blk), F32),
            pltpu.VMEM((count, rest, blk), F32),
        ],
        compiler_params=spare,
        cost_estimate=cost(0.001),
        name="late_tiles",
    )(table, weights, xo, hb, tile_sums, *late)
    other = lax.ppermute(send, "seq", swap)
    mine, *rounded = pl.pallas_call(
        pair_kernel,
        out_shape=(shape((2, blk, blk), F32),) + (shape((2, blk, blk), BF16),) * (shards - 1),
        in_specs=[vmem, vmem],
        out_specs=(vmem,) * shards,
        compiler_params=spare,
        cost_estimate=cost(0.001),
        name="pair",
    )(own, other)
    others = [
        lax.ppermute(rounded[k - 1], "fsdp", swaps(shards, k)) for k in range(shards - 1, 0, -1)
    ]

    def of_all(a):
        if n_tensor == 2:
            return [a, lax.ppermute(a, "tensor", swap)]
        everyone = lax.all_gather(a, "tensor")
        return [everyone[n] for n in range(n_tensor)]

    def block_scratch(size):
        return [
            pltpu.VMEM((size, width), BF16),
            pltpu.VMEM((size, width) if n_tensor != 2 else (8, 128), F32),
        ]

    parts = of_all(back_early)
    infos = [part[count * cut :] for part in parts]
    if n_tensor == 2:
        pass
    token_grad, rows = pl.pallas_call(
        functools.partial(place_early_kernel, n_tensor, count),
        out_shape=(shape((toks, width), BF16), shape((n_tensor, count), I32)),
        in_specs=[vmem] * (2 * n_tensor),
        out_specs=(hbm, smem),
        scratch_shapes=[
            pltpu.VMEM((n_tensor, 8, blk), I32),
            pltpu.SMEM((n_tensor, 8, blk), I32),
            pltpu.SemaphoreType.DMA,
            *block_scratch(cut),
            pltpu.SemaphoreType.DMA,
        ],
        compiler_params=spare,
        cost_estimate=cost(0.001),
        name="place_early",
    )(*infos, *parts)
    token_grad, tile_grads = pl.pallas_call(
        functools.partial(place_late_kernel, n_tensor, shards, cut, count),
        out_shape=(shape((toks, width), BF16), shape((2, blk, blk), BF16)),
        in_specs=[smem] + [vmem] * n_tensor + [hbm] + [vmem] * shards,
        out_specs=(hbm, hbm),
        scratch_shapes=[
            *block_scratch(rest),
            pltpu.SemaphoreType.DMA,
            pltpu.VMEM((2, blk, blk), BF16),
            pltpu.SemaphoreType.DMA,
        ],
        input_output_aliases={n_tensor + 1: 0},
        compiler_params=spare,
        cost_estimate=cost(0.001),
        name="place_late",
    )(rows, *of_all(back_late), token_grad, mine, *others)
    return token_grad, tile_grads.reshape(1, 1, 1, 2, blk, blk)


def solution(mesh):
    return jax.shard_map(
        functools.partial(local, dict(mesh.shape)),
        mesh=mesh,
        in_specs=(
            P(("group", "fsdp", "seq"), "tensor"),
            P(("group", "fsdp", "seq"), "tensor"),
            P("fsdp", "tensor", None, None, None, None),
            P("fsdp", "tensor", None, None),
            P("fsdp", "tensor", None),
        ),
        out_specs=(
            P(("group", "fsdp", "seq"), None),
            P(("group", "fsdp"), "tensor", "seq", None, None, None),
        ),
        check_vma=False,
    )
```

```python
import functools

import jax
import jax.numpy as jnp
from jax import lax
from jax.experimental import pallas as pl
from jax.experimental.pallas import tpu as pltpu
from jax.sharding import PartitionSpec as P

F32 = jnp.float32
BF16 = jnp.bfloat16
I32 = jnp.int32
ROW, COL, SLOT, CFIRST, RFIRST = range(5)
INFO_ROWS = 16


def shift(size, k):
    return [(i, (i + k) % size) for i in range(size)]


def swaps(size, k):
    return [(i, i ^ k) for i in range(size)]


def loop(count, body):
    if count <= 8:
        for i in range(count):
            body(i)
    else:
        lax.fori_loop(0, count, lambda i, c: (body(i), c)[1], 0)


def find_first(table, src, dst, count):
    def one(i):
        v = table[src, i]

        def step(n, best):
            at = i - 1 - n
            return jnp.where(table[src, at] == v, at, best).astype(I32)

        if isinstance(i, int):
            best = jnp.int32(i)
            for n in range(i):
                best = step(n, best)
        else:
            best = lax.fori_loop(0, i, step, i)
        table[dst, i] = best

    loop(count, one)


def cost(us):
    return pl.CostEstimate(flops=0, bytes_accessed=int(us * 3.69e6), transcendentals=0)


def dot(a, b, dims):
    return lax.dot_general(a, b, (dims, ((), ())), preferred_element_type=F32)


def pack_kernel(cols, keep, count, tiles, packed):
    _, _, cap, _, blk, _ = tiles.shape
    for j in range(cap):
        for m in range(2):
            packed[pl.ds((2 * j + m) * blk, blk), :] = tiles[0, 0, j, m]
    line = lax.broadcasted_iota(I32, (INFO_ROWS, blk), 0)
    lane = lax.broadcasted_iota(I32, (INFO_ROWS, blk), 1)
    info = jnp.zeros((INFO_ROWS, blk), I32)
    for j in range(cap):
        for m in range(2):
            b = keep[0, 0, j, m]
            r = lax.div(b, jnp.int32(cols))
            c = b - r * cols
            r = jnp.where(j < count[0, 0, m], r, -1)
            here = lane == 2 * j + m
            info = jnp.where(here & (line == 0), r, jnp.where(here & (line == 1), c, info))
    packed[pl.ds(2 * cap * blk, INFO_ROWS), :] = info.astype(F32).astype(BF16)


def prepare_kernel(shards, cap, *refs):
    packed, refs = refs[:shards], refs[shards:]
    hidden, listed, weights, hb, ints, info, table, isem, tsem, hsem = refs
    blk = weights.shape[-1]
    base = 2 * cap * blk
    count = hb.shape[0]
    live = count // 2
    for k in range(shards):
        ints[k] = packed[k][pl.ds(base, INFO_ROWS), :].astype(F32)[:8].astype(I32)
    fetch = pltpu.make_async_copy(ints, info, isem)
    fetch.start()
    fetch.wait()
    for m in range(2):
        p = jnp.int32(m * live)
        for k in range(shards):
            for j in range(cap):
                r = info[k, 0, 2 * j + m]
                table[ROW, p] = r
                table[COL, p] = info[k, 1, 2 * j + m]
                table[SLOT, p] = k * cap + j
                p = p + jnp.where(r >= 0, 1, 0).astype(I32)

    def column(i):
        at = pl.multiple_of(table[COL, i] * blk, blk)
        return pltpu.make_async_copy(hidden.at[:, pl.ds(at, blk)], hb.at[i], hsem.at[i])

    loop(count, lambda i: column(i).start())
    find_first(table, COL, CFIRST, count)
    find_first(table, ROW, RFIRST, count)
    done = pltpu.make_async_copy(table, listed, tsem)
    done.start()
    for m in range(2):
        p = jnp.int32(m * live)
        for k in range(shards):
            for j in range(cap):
                weights[p] = packed[k][pl.ds((2 * j + m) * blk, blk), :]
                p = p + jnp.where(info[k, 0, 2 * j + m] >= 0, 1, 0).astype(I32)
    loop(count, lambda i: column(i).wait())
    done.wait()


def forward_backward(lo, listed, table, tsem, weights, tokens, hb, remote, xs, pre, grads):
    fetch = pltpu.make_async_copy(listed, table, tsem)
    fetch.start()
    count, size, blk = xs.shape
    live = count // 2
    rows_here = remote[0].shape[1] // blk
    n_tensor = len(remote) + 1
    t = lax.axis_index("tensor")
    pre[...] = jnp.zeros_like(pre)
    fetch.wait()

    def forward(i):
        r = table[ROW, i]
        part = lax.rem(lax.div(r, rows_here) - t + n_tensor, n_tensor)
        at = pl.multiple_of(lax.rem(r, rows_here) * blk, blk)
        x = tokens[pl.ds(lo, size), pl.ds(at, blk)]
        for n, ref in enumerate(remote):
            x = jnp.where(part == n + 1, ref[:, pl.ds(at, blk)], x)
        xs[i] = x
        pre[i // live, table[CFIRST, i]] += dot(x, weights[i], ((1,), (0,)))

    loop(count, forward)

    def backward(i):
        m = i // live
        f = table[CFIRST, i]
        gate = pre[0, f]
        h = hb[i, pl.ds(lo, size), :].astype(F32)
        sig = 1.0 / (1.0 + jnp.exp(-gate))

        def of_gate():
            return h * pre[1, f] * sig * (1.0 + gate * (1.0 - sig))

        def of_up():
            return h * gate * sig

        if isinstance(m, int):
            grad = of_up() if m else of_gate()
        else:
            grad = jnp.where(m == 0, of_gate(), of_up())
        grads[i] = grad.astype(BF16)

    loop(count, backward)


def back_terms(table, weights, grads, acc, back):
    count, size, _ = acc.shape
    acc[...] = jnp.zeros_like(acc)

    def one(i):
        acc[table[RFIRST, i]] += dot(grads[i], weights[i], ((1,), (1,)))

    def put(i):
        back[pl.ds(pl.multiple_of(i * size, size), size), :] = acc[i].astype(BF16)

    loop(count, one)
    loop(count, put)


def first_kernel(n_tensor, listed, weights, tokens, hb, *refs):
    remote, refs = refs[: n_tensor - 1], refs[n_tensor - 1 :]
    back, tile_sums, xs, pre, grads, acc, table, tsem = refs
    forward_backward(0, listed, table, tsem, weights, tokens, hb, remote, xs, pre, grads)

    def tile(i):
        tile_sums[i] = dot(xs[i], grads[i], ((0,), (0,)))

    count, size, blk = xs.shape
    loop(count, tile)
    back_terms(table, weights, grads, acc, back)
    lane = lax.broadcasted_iota(I32, (INFO_ROWS, blk), 1)
    rows = jnp.zeros((INFO_ROWS, blk), I32)
    for i in range(count):
        rows = jnp.where(lane == i, table[ROW, i], rows)
    back[pl.ds(count * size, INFO_ROWS), :] = rows.astype(F32).astype(BF16)


def second_kernel(n_tensor, lo, cap, listed, weights, tokens, hb, tile_sums, *refs):
    remote, refs = refs[: n_tensor - 1], refs[n_tensor - 1 :]
    own, send, back, grads, xs, pre, both, acc, table, tsem = refs
    both[...] = jnp.zeros_like(both)
    forward_backward(lo, listed, table, tsem, weights, tokens, hb, remote, xs, pre, grads)
    s = lax.axis_index("seq")
    live = xs.shape[0] // 2

    def tile(i):
        value = tile_sums[i] + dot(xs[i], grads[i], ((0,), (0,)))
        slot = table[SLOT, i]
        both[lax.rem(slot + s, cap), lax.div(slot, cap), i // live] = value

    loop(xs.shape[0], tile)
    own[...] = both[0]
    send[...] = both[1].astype(send.dtype)
    back_terms(table, weights, grads, acc, back)


def pair_kernel(own, other, *sums):
    for k, total in enumerate(sums):
        total[...] = (own[k] + other[k].astype(F32)).astype(total.dtype)


def place_chunk(n_tensor, count, lo, refs, meanwhile=None):
    infos, refs = refs[:n_tensor], refs[n_tensor:]
    parts, refs = refs[:n_tensor], refs[n_tensor:]
    out, ints, rows, isem, block, wide, sem = refs
    size = block.shape[0]
    blk = parts[0].shape[1]
    for n, info in enumerate(infos):
        ints[n] = info[...].astype(F32)[:8].astype(I32)
    fetch = pltpu.make_async_copy(ints, rows, isem)
    fetch.start()
    total = block if n_tensor == 2 else wide
    total[...] = jnp.zeros_like(total)
    if meanwhile is not None:
        meanwhile()
    fetch.wait()
    for n, part in enumerate(parts):

        def add(i):
            at = pl.ds(pl.multiple_of(rows[n, 0, i] * blk, blk), blk)
            term = part[pl.ds(pl.multiple_of(i * size, size), size), :].astype(F32)
            total[:, at] = (total[:, at].astype(F32) + term).astype(total.dtype)

        loop(count, add)
    if n_tensor != 2:
        block[...] = wide[...].astype(BF16)
    copy = pltpu.make_async_copy(block, out.at[pl.ds(lo, size), :], sem)
    copy.start()
    copy.wait()


def place_early_kernel(n_tensor, count, *refs):
    place_chunk(n_tensor, count, 0, refs)


def place_late_kernel(n_tensor, shards, lo, count, *refs):
    first, refs = refs[: 2 * n_tensor], refs[2 * n_tensor :]
    _, mine, *others = refs[: shards + 1]
    out, tile_grads, *scratch, tile_sum, tile_sem = refs[shards + 1 :]
    tile_copy = pltpu.make_async_copy(tile_sum, tile_grads, tile_sem)

    def add_tiles():
        total = mine[...]
        for other in others:
            total = total + other[...].astype(F32)
        tile_sum[...] = total.astype(BF16)
        tile_copy.start()

    place_chunk(n_tensor, count, lo, (*first, out, *scratch), add_tiles)
    tile_copy.wait()


def local(sizes, tokens, hidden_grad, tile_blocks, tile_keep, tile_count):
    shards, n_tensor = sizes["fsdp"], sizes["tensor"]
    blk = tile_blocks.shape[-1]
    cap = tile_blocks.shape[2]
    toks = tokens.shape[0]
    width = tokens.shape[1] * n_tensor
    cols = hidden_grad.shape[1] // blk
    count = shards * cap
    cut = toks * 13 // 16 // 16 * 16
    rest = toks - cut
    vmem = pl.BlockSpec(memory_space=pltpu.VMEM)
    smem = pl.BlockSpec(memory_space=pltpu.SMEM)
    hbm = pl.BlockSpec(memory_space=pltpu.HBM)
    spare = pltpu.CompilerParams(vmem_limit_bytes=(16 if count <= 8 else 40) * 2**20)
    swap = shift(2, 1)
    order = [shards // 2] + [k for k in range(shards - 1, 0, -1) if k != shards // 2]

    def shape(dims, kind):
        return jax.ShapeDtypeStruct(dims, kind)

    def to_partners(a):
        return [
            lax.ppermute(a, "tensor", shift(n_tensor, n_tensor - k)) for k in range(1, n_tensor)
        ]

    early = to_partners(tokens[:cut])
    packed = pl.pallas_call(
        functools.partial(pack_kernel, cols),
        out_shape=shape((2 * cap * blk + INFO_ROWS, blk), BF16),
        in_specs=[smem, smem, vmem],
        out_specs=vmem,
        compiler_params=spare,
        cost_estimate=cost(0.001),
        name="pack",
    )(tile_keep, tile_count, tile_blocks)
    late = to_partners(tokens[cut:])
    gathered = [packed] + [
        lax.ppermute(packed, "fsdp", swaps(shards, k)) for k in range(1, shards)
    ]

    listed, weights, hb = pl.pallas_call(
        functools.partial(prepare_kernel, shards, cap),
        out_shape=(
            shape((8, blk), I32),
            shape((count + 1, blk, blk), BF16),
            shape((count, toks, blk), BF16),
        ),
        in_specs=[vmem] * shards + [hbm],
        out_specs=(vmem, vmem, vmem),
        scratch_shapes=[
            pltpu.VMEM((shards, 8, blk), I32),
            pltpu.SMEM((shards, 8, blk), I32),
            pltpu.SMEM((8, blk), I32),
            pltpu.SemaphoreType.DMA,
            pltpu.SemaphoreType.DMA,
            pltpu.SemaphoreType.DMA((count,)),
        ],
        compiler_params=pltpu.CompilerParams(vmem_limit_bytes=50 * 2**20),
        cost_estimate=cost(0.001),
        name="prepare",
    )(*gathered, hidden_grad)

    back_early, tile_sums = pl.pallas_call(
        functools.partial(first_kernel, n_tensor),
        out_shape=(shape((count * cut + INFO_ROWS, blk), BF16), shape((count, blk, blk), F32)),
        in_specs=[vmem] * (3 + n_tensor),
        out_specs=(vmem, vmem),
        scratch_shapes=[
            pltpu.VMEM((count, cut, blk), BF16),
            pltpu.VMEM((2, count, cut, blk), F32),
            pltpu.VMEM((count, cut, blk), BF16),
            pltpu.VMEM((count, cut, blk), F32),
            pltpu.SMEM((8, blk), I32),
            pltpu.SemaphoreType.DMA,
        ],
        compiler_params=spare,
        cost_estimate=cost(0.001),
        name="early_terms",
    )(listed, weights, tokens, hb, *early)

    own, send, back_late = pl.pallas_call(
        functools.partial(second_kernel, n_tensor, cut, cap),
        out_shape=(
            shape((shards, 2, blk, blk), F32),
            shape((shards, 2, blk, blk), BF16),
            shape((count * rest, blk), BF16),
        ),
        in_specs=[vmem] * (4 + n_tensor),
        out_specs=(vmem,) * 3,
        scratch_shapes=[
            pltpu.VMEM((count, rest, blk), BF16),
            pltpu.VMEM((count, rest, blk), BF16),
            pltpu.VMEM((2, count, rest, blk), F32),
            pltpu.VMEM((cap, shards, 2, blk, blk), F32),
            pltpu.VMEM((count, rest, blk), F32),
            pltpu.SMEM((8, blk), I32),
            pltpu.SemaphoreType.DMA,
        ],
        compiler_params=spare,
        cost_estimate=cost(0.001),
        name="late_tiles",
    )(listed, weights, tokens, hb, tile_sums, *late)
    other = lax.ppermute(send, "seq", swap)
    mine, *rounded = pl.pallas_call(
        pair_kernel,
        out_shape=(shape((2, blk, blk), F32),) + (shape((2, blk, blk), BF16),) * (shards - 1),
        in_specs=[vmem, vmem],
        out_specs=(vmem,) * shards,
        compiler_params=spare,
        cost_estimate=cost(0.001),
        name="pair",
    )(own, other)
    others = [
        lax.ppermute(rounded[k - 1], "fsdp", swaps(shards, k)) for k in order
    ]

    def of_all(a):
        if n_tensor == 2:
            return [a, lax.ppermute(a, "tensor", swap)]
        everyone = lax.all_gather(a, "tensor")
        return [everyone[n] for n in range(n_tensor)]

    def scratch(size):
        return [
            pltpu.VMEM((n_tensor, 8, blk), I32),
            pltpu.SMEM((n_tensor, 8, blk), I32),
            pltpu.SemaphoreType.DMA,
            pltpu.VMEM((size, width), BF16),
            pltpu.VMEM((size, width) if n_tensor != 2 else (8, 128), F32),
            pltpu.SemaphoreType.DMA,
        ]

    parts = of_all(back_early)
    infos = [part[count * cut :] for part in parts]
    token_grad = pl.pallas_call(
        functools.partial(place_early_kernel, n_tensor, count),
        out_shape=shape((toks, width), BF16),
        in_specs=[vmem] * (2 * n_tensor),
        out_specs=hbm,
        scratch_shapes=scratch(cut),
        compiler_params=spare,
        cost_estimate=cost(0.001),
        name="place_early",
    )(*infos, *parts)
    token_grad, tile_grads = pl.pallas_call(
        functools.partial(place_late_kernel, n_tensor, shards, cut, count),
        out_shape=(shape((toks, width), BF16), shape((2, blk, blk), BF16)),
        in_specs=[vmem] * (2 * n_tensor) + [hbm] + [vmem] * shards,
        out_specs=(hbm, hbm),
        scratch_shapes=[
            *scratch(rest),
            pltpu.VMEM((2, blk, blk), BF16),
            pltpu.SemaphoreType.DMA,
        ],
        input_output_aliases={2 * n_tensor: 0},
        compiler_params=spare,
        cost_estimate=cost(0.001),
        name="place_late",
    )(*infos, *of_all(back_late), token_grad, mine, *others)
    return token_grad, tile_grads.reshape(1, 1, 1, 2, blk, blk)


def solution(mesh):
    return jax.shard_map(
        functools.partial(local, dict(mesh.shape)),
        mesh=mesh,
        in_specs=(
            P(("group", "fsdp", "seq"), "tensor"),
            P(("group", "fsdp", "seq"), "tensor"),
            P("fsdp", "tensor", None, None, None, None),
            P("fsdp", "tensor", None, None),
            P("fsdp", "tensor", None),
        ),
        out_specs=(
            P(("group", "fsdp", "seq"), None),
            P(("group", "fsdp"), "tensor", "seq", None, None, None),
        ),
        check_vma=False,
    )
```

```python
import functools

import jax
import jax.numpy as jnp
from jax import lax
from jax.experimental import pallas as pl
from jax.experimental.pallas import tpu as pltpu
from jax.sharding import PartitionSpec as P

F32 = jnp.float32
BF16 = jnp.bfloat16
I32 = jnp.int32
ROW, COL, SLOT, CFIRST, RFIRST = range(5)
INFO_ROWS = 16


def shift(size, k):
    return [(i, (i + k) % size) for i in range(size)]


def swaps(size, k):
    return [(i, i ^ k) for i in range(size)]


def loop(count, body):
    if count <= 8:
        for i in range(count):
            body(i)
    else:
        lax.fori_loop(0, count, lambda i, c: (body(i), c)[1], 0)


def find_first(table, src, dst, count):
    def one(i):
        v = table[i, src]

        def step(n, best):
            at = i - 1 - n
            return jnp.where(table[at, src] == v, at, best).astype(I32)

        if isinstance(i, int):
            best = jnp.int32(i)
            for n in range(i):
                best = step(n, best)
        else:
            best = lax.fori_loop(0, i, step, i)
        table[i, dst] = best

    loop(count, one)


def cost(us):
    return pl.CostEstimate(flops=0, bytes_accessed=int(us * 3.69e6), transcendentals=0)


def dot(a, b, dims):
    return lax.dot_general(a, b, (dims, ((), ())), preferred_element_type=F32)


def pack_kernel(cols, keep, count, tiles, packed):
    _, _, cap, _, blk, _ = tiles.shape
    for j in range(cap):
        for m in range(2):
            packed[pl.ds((2 * j + m) * blk, blk), :] = tiles[0, 0, j, m]
    line = lax.broadcasted_iota(I32, (INFO_ROWS, blk), 0)
    lane = lax.broadcasted_iota(I32, (INFO_ROWS, blk), 1)
    info = jnp.zeros((INFO_ROWS, blk), I32)
    for j in range(cap):
        for m in range(2):
            b = keep[0, 0, j, m]
            r = lax.div(b, jnp.int32(cols))
            c = b - r * cols
            r = jnp.where(j < count[0, 0, m], r, -1)
            here = lane == 2 * j + m
            info = jnp.where(here & (line == 0), r, jnp.where(here & (line == 1), c, info))
    packed[pl.ds(2 * cap * blk, INFO_ROWS), :] = info.astype(F32).astype(BF16)


def prepare_kernel(shards, cap, *refs):
    packed, refs = refs[:shards], refs[shards:]
    hidden, listed, weights, hb, info, table, tsem, hsem = refs
    blk = weights.shape[-1]
    base = 2 * cap * blk
    count = hb.shape[0]
    live = count // 2
    for k in range(shards):
        info[k] = packed[k][pl.ds(base, INFO_ROWS), :].astype(F32)[:8].astype(I32)
    for m in range(2):
        p = jnp.int32(m * live)
        for k in range(shards):
            for j in range(cap):
                r = info[k, 0, 2 * j + m]
                table[p, ROW] = r
                table[p, COL] = info[k, 1, 2 * j + m]
                table[p, SLOT] = k * cap + j
                p = p + jnp.where(r >= 0, 1, 0).astype(I32)

    def column(i):
        at = pl.multiple_of(table[i, COL] * blk, blk)
        return pltpu.make_async_copy(hidden.at[:, pl.ds(at, blk)], hb.at[i], hsem.at[i])

    loop(count, lambda i: column(i).start())
    find_first(table, COL, CFIRST, count)
    find_first(table, ROW, RFIRST, count)
    done = pltpu.make_async_copy(table, listed, tsem)
    done.start()
    for m in range(2):
        p = jnp.int32(m * live)
        for k in range(shards):
            for j in range(cap):
                weights[p] = packed[k][pl.ds((2 * j + m) * blk, blk), :]
                p = p + jnp.where(info[k, 0, 2 * j + m] >= 0, 1, 0).astype(I32)
    loop(count, lambda i: column(i).wait())
    done.wait()


def forward_backward(lo, table, weights, tokens, hb, remote, xs, pre, grads):
    count, size, blk = xs.shape
    live = count // 2
    rows_here = remote[0].shape[1] // blk
    n_tensor = len(remote) + 1
    t = lax.axis_index("tensor")
    pre[...] = jnp.zeros_like(pre)

    def forward(i):
        r = table[i, ROW]
        part = lax.rem(lax.div(r, rows_here) - t + n_tensor, n_tensor)
        at = pl.multiple_of(lax.rem(r, rows_here) * blk, blk)
        x = tokens[pl.ds(lo, size), pl.ds(at, blk)]
        for n, ref in enumerate(remote):
            x = jnp.where(part == n + 1, ref[:, pl.ds(at, blk)], x)
        xs[i] = x
        pre[i // live, table[i, CFIRST]] += dot(x, weights[i], ((1,), (0,)))

    loop(count, forward)

    def backward(i):
        m = i // live
        f = table[i, CFIRST]
        gate = pre[0, f]
        h = hb[i, pl.ds(lo, size), :].astype(F32)
        sig = 1.0 / (1.0 + jnp.exp(-gate))

        def of_gate():
            return h * pre[1, f] * sig * (1.0 + gate * (1.0 - sig))

        def of_up():
            return h * gate * sig

        if isinstance(m, int):
            grad = of_up() if m else of_gate()
        else:
            grad = jnp.where(m == 0, of_gate(), of_up())
        grads[i] = grad.astype(BF16)

    loop(count, backward)


def back_terms(table, weights, grads, acc, back):
    count, size, _ = acc.shape
    acc[...] = jnp.zeros_like(acc)

    def one(i):
        acc[table[i, RFIRST]] += dot(grads[i], weights[i], ((1,), (1,)))

    def put(i):
        back[pl.ds(pl.multiple_of(i * size, size), size), :] = acc[i].astype(BF16)

    loop(count, one)
    loop(count, put)


def first_kernel(n_tensor, table, weights, tokens, hb, *refs):
    remote, refs = refs[: n_tensor - 1], refs[n_tensor - 1 :]
    back, tile_sums, xs, pre, grads, acc = refs
    forward_backward(0, table, weights, tokens, hb, remote, xs, pre, grads)

    def tile(i):
        tile_sums[i] = dot(xs[i], grads[i], ((0,), (0,)))

    count, size, blk = xs.shape
    loop(count, tile)
    back_terms(table, weights, grads, acc, back)
    lines = back.shape[0] - count * size
    line = lax.broadcasted_iota(I32, (lines, blk), 0)
    rows = jnp.zeros((lines, blk), I32)
    for i in range(count):
        rows = jnp.where(line == i, table[i, ROW], rows)
    back[pl.ds(count * size, lines), :] = rows.astype(F32).astype(BF16)


def second_kernel(n_tensor, lo, cap, table, weights, tokens, hb, tile_sums, *refs):
    remote, refs = refs[: n_tensor - 1], refs[n_tensor - 1 :]
    own, send, back, grads, xs, pre, both, acc = refs
    both[...] = jnp.zeros_like(both)
    forward_backward(lo, table, weights, tokens, hb, remote, xs, pre, grads)
    s = lax.axis_index("seq")
    live = xs.shape[0] // 2

    def tile(i):
        value = tile_sums[i] + dot(xs[i], grads[i], ((0,), (0,)))
        slot = table[i, SLOT]
        both[lax.rem(slot + s, cap), lax.div(slot, cap), i // live] = value

    loop(xs.shape[0], tile)
    own[...] = both[0]
    send[...] = both[1].astype(send.dtype)
    back_terms(table, weights, grads, acc, back)


def pair_kernel(own, other, *sums):
    for k, total in enumerate(sums):
        total[...] = (own[k] + other[k].astype(F32)).astype(total.dtype)


def place_chunk(n_tensor, count, lo, refs, meanwhile=None):
    infos, refs = refs[:n_tensor], refs[n_tensor:]
    parts, refs = refs[:n_tensor], refs[n_tensor:]
    out, rows, block, wide, sem = refs
    size = block.shape[0]
    blk = parts[0].shape[1]
    for n, info in enumerate(infos):
        rows[n] = info[...].astype(F32).astype(I32)
    total = block if n_tensor == 2 else wide
    total[...] = jnp.zeros_like(total)
    if meanwhile is not None:
        meanwhile()
    for n, part in enumerate(parts):

        def add(i):
            at = pl.ds(pl.multiple_of(rows[n, i, 0] * blk, blk), blk)
            term = part[pl.ds(pl.multiple_of(i * size, size), size), :].astype(F32)
            total[:, at] = (total[:, at].astype(F32) + term).astype(total.dtype)

        loop(count, add)
    if n_tensor != 2:
        block[...] = wide[...].astype(BF16)
    copy = pltpu.make_async_copy(block, out.at[pl.ds(lo, size), :], sem)
    copy.start()
    copy.wait()


def place_early_kernel(n_tensor, count, *refs):
    place_chunk(n_tensor, count, 0, refs)


def place_late_kernel(n_tensor, shards, lo, count, *refs):
    first, refs = refs[: 2 * n_tensor], refs[2 * n_tensor :]
    _, mine, *others = refs[: shards + 1]
    out, tile_grads, *scratch, tile_sum, tile_sem = refs[shards + 1 :]
    tile_copy = pltpu.make_async_copy(tile_sum, tile_grads, tile_sem)

    def add_tiles():
        total = mine[...]
        for other in others:
            total = total + other[...].astype(F32)
        tile_sum[...] = total.astype(BF16)
        tile_copy.start()

    place_chunk(n_tensor, count, lo, (*first, out, *scratch), add_tiles)
    tile_copy.wait()


def local(sizes, tokens, hidden_grad, tile_blocks, tile_keep, tile_count):
    shards, n_tensor = sizes["fsdp"], sizes["tensor"]
    blk = tile_blocks.shape[-1]
    cap = tile_blocks.shape[2]
    toks = tokens.shape[0]
    width = tokens.shape[1] * n_tensor
    cols = hidden_grad.shape[1] // blk
    count = shards * cap
    cut = toks * 13 // 16 // 16 * 16
    rest = toks - cut
    lines = (count // 16 + 1) * 16
    vmem = pl.BlockSpec(memory_space=pltpu.VMEM)
    smem = pl.BlockSpec(memory_space=pltpu.SMEM)
    hbm = pl.BlockSpec(memory_space=pltpu.HBM)
    spare = pltpu.CompilerParams(vmem_limit_bytes=(16 if count <= 8 else 40) * 2**20)
    swap = shift(2, 1)
    order = [shards // 2] + [k for k in range(shards - 1, 0, -1) if k != shards // 2]

    def shape(dims, kind):
        return jax.ShapeDtypeStruct(dims, kind)

    def to_partners(a):
        return [
            lax.ppermute(a, "tensor", shift(n_tensor, n_tensor - k)) for k in range(1, n_tensor)
        ]

    early = to_partners(tokens[:cut])
    packed = pl.pallas_call(
        functools.partial(pack_kernel, cols),
        out_shape=shape((2 * cap * blk + INFO_ROWS, blk), BF16),
        in_specs=[smem, smem, vmem],
        out_specs=vmem,
        compiler_params=spare,
        cost_estimate=cost(0.001),
        name="pack",
    )(tile_keep, tile_count, tile_blocks)
    late = to_partners(tokens[cut:])
    gathered = [packed] + [
        lax.ppermute(packed, "fsdp", swaps(shards, k)) for k in range(1, shards)
    ]

    listed, weights, hb = pl.pallas_call(
        functools.partial(prepare_kernel, shards, cap),
        out_shape=(
            shape((lines, blk), I32),
            shape((count + 1, blk, blk), BF16),
            shape((count, toks, blk), BF16),
        ),
        in_specs=[vmem] * shards + [hbm],
        out_specs=(vmem, vmem, vmem),
        scratch_shapes=[
            pltpu.VMEM((shards, 8, blk), I32),
            pltpu.SMEM((lines, blk), I32),
            pltpu.SemaphoreType.DMA,
            pltpu.SemaphoreType.DMA((count,)),
        ],
        compiler_params=pltpu.CompilerParams(vmem_limit_bytes=50 * 2**20),
        cost_estimate=cost(0.001),
        name="prepare",
    )(*gathered, hidden_grad)

    back_early, tile_sums = pl.pallas_call(
        functools.partial(first_kernel, n_tensor),
        out_shape=(shape((count * cut + lines, blk), BF16), shape((count, blk, blk), F32)),
        in_specs=[vmem] * (3 + n_tensor),
        out_specs=(vmem, vmem),
        scratch_shapes=[
            pltpu.VMEM((count, cut, blk), BF16),
            pltpu.VMEM((2, count, cut, blk), F32),
            pltpu.VMEM((count, cut, blk), BF16),
            pltpu.VMEM((count, cut, blk), F32),
        ],
        compiler_params=spare,
        cost_estimate=cost(0.001),
        name="early_terms",
    )(listed, weights, tokens, hb, *early)

    own, send, back_late = pl.pallas_call(
        functools.partial(second_kernel, n_tensor, cut, cap),
        out_shape=(
            shape((shards, 2, blk, blk), F32),
            shape((shards, 2, blk, blk), BF16),
            shape((count * rest, blk), BF16),
        ),
        in_specs=[vmem] * (4 + n_tensor),
        out_specs=(vmem,) * 3,
        scratch_shapes=[
            pltpu.VMEM((count, rest, blk), BF16),
            pltpu.VMEM((count, rest, blk), BF16),
            pltpu.VMEM((2, count, rest, blk), F32),
            pltpu.VMEM((cap, shards, 2, blk, blk), F32),
            pltpu.VMEM((count, rest, blk), F32),
        ],
        compiler_params=spare,
        cost_estimate=cost(0.001),
        name="late_tiles",
    )(listed, weights, tokens, hb, tile_sums, *late)
    other = lax.ppermute(send, "seq", swap)
    mine, *rounded = pl.pallas_call(
        pair_kernel,
        out_shape=(shape((2, blk, blk), F32),) + (shape((2, blk, blk), BF16),) * (shards - 1),
        in_specs=[vmem, vmem],
        out_specs=(vmem,) * shards,
        compiler_params=spare,
        cost_estimate=cost(0.001),
        name="pair",
    )(own, other)
    others = [
        lax.ppermute(rounded[k - 1], "fsdp", swaps(shards, k)) for k in order
    ]

    def of_all(a):
        if n_tensor == 2:
            return [a, lax.ppermute(a, "tensor", swap)]
        everyone = lax.all_gather(a, "tensor")
        return [everyone[n] for n in range(n_tensor)]

    def scratch(size):
        return [
            pltpu.VMEM((n_tensor, lines, blk), I32),
            pltpu.VMEM((size, width), BF16),
            pltpu.VMEM((size, width) if n_tensor != 2 else (8, 128), F32),
            pltpu.SemaphoreType.DMA,
        ]

    parts = of_all(back_early)
    infos = [part[count * cut :] for part in parts]
    token_grad = pl.pallas_call(
        functools.partial(place_early_kernel, n_tensor, count),
        out_shape=shape((toks, width), BF16),
        in_specs=[vmem] * (2 * n_tensor),
        out_specs=hbm,
        scratch_shapes=scratch(cut),
        compiler_params=spare,
        cost_estimate=cost(0.001),
        name="place_early",
    )(*infos, *parts)
    token_grad, tile_grads = pl.pallas_call(
        functools.partial(place_late_kernel, n_tensor, shards, cut, count),
        out_shape=(shape((toks, width), BF16), shape((2, blk, blk), BF16)),
        in_specs=[vmem] * (2 * n_tensor) + [hbm] + [vmem] * shards,
        out_specs=(hbm, hbm),
        scratch_shapes=[
            *scratch(rest),
            pltpu.VMEM((2, blk, blk), BF16),
            pltpu.SemaphoreType.DMA,
        ],
        input_output_aliases={2 * n_tensor: 0},
        compiler_params=spare,
        cost_estimate=cost(0.001),
        name="place_late",
    )(*infos, *of_all(back_late), token_grad, mine, *others)
    return token_grad, tile_grads.reshape(1, 1, 1, 2, blk, blk)


def solution(mesh):
    return jax.shard_map(
        functools.partial(local, dict(mesh.shape)),
        mesh=mesh,
        in_specs=(
            P(("group", "fsdp", "seq"), "tensor"),
            P(("group", "fsdp", "seq"), "tensor"),
            P("fsdp", "tensor", None, None, None, None),
            P("fsdp", "tensor", None, None),
            P("fsdp", "tensor", None),
        ),
        out_specs=(
            P(("group", "fsdp", "seq"), None),
            P(("group", "fsdp"), "tensor", "seq", None, None, None),
        ),
        check_vma=False,
    )
```

```python
import functools

import jax
import jax.numpy as jnp
from jax import lax
from jax.experimental import pallas as pl
from jax.experimental.pallas import tpu as pltpu
from jax.sharding import PartitionSpec as P

F32 = jnp.float32
BF16 = jnp.bfloat16
I32 = jnp.int32
ROW, COL, SLOT, CFIRST, RFIRST = range(5)
INFO_ROWS = 16


def shift(size, k):
    return [(i, (i + k) % size) for i in range(size)]


def swaps(size, k):
    return [(i, i ^ k) for i in range(size)]


def loop(count, body):
    if count <= 8:
        for i in range(count):
            body(i)
    else:
        lax.fori_loop(0, count, lambda i, c: (body(i), c)[1], 0)


def find_first(table, src, dst, count):
    def one(i):
        v = table[i, src]

        def step(n, best):
            at = i - 1 - n
            return jnp.where(table[at, src] == v, at, best).astype(I32)

        if isinstance(i, int):
            best = jnp.int32(i)
            for n in range(i):
                best = step(n, best)
        else:
            best = lax.fori_loop(0, i, step, i)
        table[i, dst] = best

    loop(count, one)


def cost(us):
    return pl.CostEstimate(flops=0, bytes_accessed=int(us * 3.69e6), transcendentals=0)


def dot(a, b, dims):
    return lax.dot_general(a, b, (dims, ((), ())), preferred_element_type=F32)


def pack_kernel(cols, keep, count, tiles, packed):
    _, _, cap, _, blk, _ = tiles.shape
    for j in range(cap):
        for m in range(2):
            packed[pl.ds((2 * j + m) * blk, blk), :] = tiles[0, 0, j, m]
    line = lax.broadcasted_iota(I32, (INFO_ROWS, blk), 0)
    lane = lax.broadcasted_iota(I32, (INFO_ROWS, blk), 1)
    info = jnp.zeros((INFO_ROWS, blk), I32)
    for j in range(cap):
        for m in range(2):
            b = keep[0, 0, j, m]
            r = lax.div(b, jnp.int32(cols))
            c = b - r * cols
            r = jnp.where(j < count[0, 0, m], r, -1)
            here = lane == 2 * j + m
            info = jnp.where(here & (line == 0), r, jnp.where(here & (line == 1), c, info))
    packed[pl.ds(2 * cap * blk, INFO_ROWS), :] = info.astype(F32).astype(BF16)


def prepare_kernel(shards, cap, *refs):
    packed, refs = refs[:shards], refs[shards:]
    hidden, listed, weights, hb, info, table, tsem, hsem = refs
    blk = weights.shape[-1]
    base = 2 * cap * blk
    count = hb.shape[0]
    live = count // 2
    for k in range(shards):
        info[k] = packed[k][pl.ds(base, INFO_ROWS), :].astype(F32)[:8].astype(I32)
    for m in range(2):
        p = jnp.int32(m * live)
        for k in range(shards):
            for j in range(cap):
                r = info[k, 0, 2 * j + m]
                table[p, ROW] = r
                table[p, COL] = info[k, 1, 2 * j + m]
                table[p, SLOT] = k * cap + j
                p = p + jnp.where(r >= 0, 1, 0).astype(I32)

    def column(i):
        at = pl.multiple_of(table[i, COL] * blk, blk)
        return pltpu.make_async_copy(hidden.at[:, pl.ds(at, blk)], hb.at[i], hsem.at[i])

    loop(count, lambda i: column(i).start())
    find_first(table, COL, CFIRST, count)
    find_first(table, ROW, RFIRST, count)
    done = pltpu.make_async_copy(table, listed, tsem)
    done.start()
    for m in range(2):
        p = jnp.int32(m * live)
        for k in range(shards):
            for j in range(cap):
                weights[p] = packed[k][pl.ds((2 * j + m) * blk, blk), :]
                p = p + jnp.where(info[k, 0, 2 * j + m] >= 0, 1, 0).astype(I32)
    loop(count, lambda i: column(i).wait())
    done.wait()


def forward_backward(lo, table, weights, tokens, hb, remote, xs, pre, grads):
    count, size, blk = xs.shape
    live = count // 2
    rows_here = remote[0].shape[1] // blk
    n_tensor = len(remote) + 1
    t = lax.axis_index("tensor")
    pre[...] = jnp.zeros_like(pre)

    def forward(i):
        r = table[i, ROW]
        part = lax.rem(lax.div(r, rows_here) - t + n_tensor, n_tensor)
        at = pl.multiple_of(lax.rem(r, rows_here) * blk, blk)
        x = tokens[pl.ds(lo, size), pl.ds(at, blk)]
        for n, ref in enumerate(remote):
            x = jnp.where(part == n + 1, ref[:, pl.ds(at, blk)], x)
        xs[i] = x
        pre[i // live, table[i, CFIRST]] += dot(x, weights[i], ((1,), (0,)))

    loop(count, forward)

    def backward(i):
        m = i // live
        f = table[i, CFIRST]
        gate = pre[0, f]
        h = hb[i, pl.ds(lo, size), :].astype(F32)
        sig = 1.0 / (1.0 + jnp.exp(-gate))

        def of_gate():
            return h * pre[1, f] * sig * (1.0 + gate * (1.0 - sig))

        def of_up():
            return h * gate * sig

        if isinstance(m, int):
            grad = of_up() if m else of_gate()
        else:
            grad = jnp.where(m == 0, of_gate(), of_up())
        grads[i] = grad.astype(BF16)

    loop(count, backward)


def back_terms(table, weights, grads, acc, back):
    count, size, _ = acc.shape
    acc[...] = jnp.zeros_like(acc)

    def one(i):
        acc[table[i, RFIRST]] += dot(grads[i], weights[i], ((1,), (1,)))

    def put(i):
        back[pl.ds(pl.multiple_of(i * size, size), size), :] = acc[i].astype(BF16)

    loop(count, one)
    loop(count, put)


def first_kernel(n_tensor, table, weights, tokens, hb, *refs):
    remote, refs = refs[: n_tensor - 1], refs[n_tensor - 1 :]
    back, tile_sums, xs, pre, grads, acc = refs
    forward_backward(0, table, weights, tokens, hb, remote, xs, pre, grads)

    def tile(i):
        tile_sums[i] = dot(xs[i], grads[i], ((0,), (0,)))

    count, size, blk = xs.shape
    loop(count, tile)
    back_terms(table, weights, grads, acc, back)
    lines = back.shape[0] - count * size
    line = lax.broadcasted_iota(I32, (lines, blk), 0)
    rows = jnp.zeros((lines, blk), I32)
    for i in range(count):
        rows = jnp.where(line == i, table[i, ROW], rows)
    back[pl.ds(count * size, lines), :] = rows.astype(F32).astype(BF16)


def second_kernel(n_tensor, lo, cap, table, weights, tokens, hb, tile_sums, *refs):
    remote, refs = refs[: n_tensor - 1], refs[n_tensor - 1 :]
    own, send, back, grads, xs, pre, both, acc = refs
    both[...] = jnp.zeros_like(both)
    forward_backward(lo, table, weights, tokens, hb, remote, xs, pre, grads)
    s = lax.axis_index("seq")
    live = xs.shape[0] // 2

    def tile(i):
        value = tile_sums[i] + dot(xs[i], grads[i], ((0,), (0,)))
        slot = table[i, SLOT]
        both[lax.rem(slot + s, cap), lax.div(slot, cap), i // live] = value

    loop(xs.shape[0], tile)
    own[...] = both[0]
    send[...] = both[1].astype(send.dtype)
    back_terms(table, weights, grads, acc, back)


def pair_kernel(own, other, *sums):
    for k, total in enumerate(sums):
        total[...] = (own[k] + other[k].astype(F32)).astype(total.dtype)


def place_chunk(n_tensor, count, lo, refs, meanwhile=None):
    infos, refs = refs[:n_tensor], refs[n_tensor:]
    parts, refs = refs[:n_tensor], refs[n_tensor:]
    out, rows, block, wide, sem = refs
    size = block.shape[0]
    blk = parts[0].shape[1]
    for n, info in enumerate(infos):
        rows[n] = info[...].astype(F32).astype(I32)
    total = block if n_tensor == 2 else wide
    total[...] = jnp.zeros_like(total)
    if meanwhile is not None:
        meanwhile()
    for n, part in enumerate(parts):

        def add(i):
            at = pl.ds(pl.multiple_of(rows[n, i, 0] * blk, blk), blk)
            term = part[pl.ds(pl.multiple_of(i * size, size), size), :].astype(F32)
            total[:, at] = (total[:, at].astype(F32) + term).astype(total.dtype)

        loop(count, add)
    if n_tensor != 2:
        block[...] = wide[...].astype(BF16)
    copy = pltpu.make_async_copy(block, out.at[pl.ds(lo, size), :], sem)
    copy.start()
    copy.wait()


def place_early_kernel(n_tensor, count, *refs):
    place_chunk(n_tensor, count, 0, refs)


def place_late_kernel(n_tensor, lo, count, *refs):
    first, (_, *rest) = refs[: 2 * n_tensor], refs[2 * n_tensor :]
    place_chunk(n_tensor, count, lo, (*first, *rest))


def sum_kernel(mine, *refs):
    *others, tile_grads = refs
    total = mine[...]
    for other in others:
        total = total + other[...].astype(F32)
    tile_grads[...] = total.astype(BF16)


def local(sizes, tokens, hidden_grad, tile_blocks, tile_keep, tile_count):
    shards, n_tensor = sizes["fsdp"], sizes["tensor"]
    blk = tile_blocks.shape[-1]
    cap = tile_blocks.shape[2]
    toks = tokens.shape[0]
    width = tokens.shape[1] * n_tensor
    cols = hidden_grad.shape[1] // blk
    count = shards * cap
    cut = toks * 13 // 16 // 16 * 16
    rest = toks - cut
    lines = (count // 16 + 1) * 16
    vmem = pl.BlockSpec(memory_space=pltpu.VMEM)
    smem = pl.BlockSpec(memory_space=pltpu.SMEM)
    hbm = pl.BlockSpec(memory_space=pltpu.HBM)
    spare = pltpu.CompilerParams(vmem_limit_bytes=(16 if count <= 8 else 40) * 2**20)
    swap = shift(2, 1)
    order = [shards // 2] + [k for k in range(shards - 1, 0, -1) if k != shards // 2]

    def shape(dims, kind):
        return jax.ShapeDtypeStruct(dims, kind)

    def to_partners(a):
        return [
            lax.ppermute(a, "tensor", shift(n_tensor, n_tensor - k)) for k in range(1, n_tensor)
        ]

    early = to_partners(tokens[:cut])
    packed = pl.pallas_call(
        functools.partial(pack_kernel, cols),
        out_shape=shape((2 * cap * blk + INFO_ROWS, blk), BF16),
        in_specs=[smem, smem, vmem],
        out_specs=vmem,
        compiler_params=spare,
        cost_estimate=cost(0.001),
        name="pack",
    )(tile_keep, tile_count, tile_blocks)
    late = to_partners(tokens[cut:])
    gathered = [packed] + [
        lax.ppermute(packed, "fsdp", swaps(shards, k)) for k in range(1, shards)
    ]

    listed, weights, hb = pl.pallas_call(
        functools.partial(prepare_kernel, shards, cap),
        out_shape=(
            shape((lines, blk), I32),
            shape((count + 1, blk, blk), BF16),
            shape((count, toks, blk), BF16),
        ),
        in_specs=[vmem] * shards + [hbm],
        out_specs=(vmem, vmem, vmem),
        scratch_shapes=[
            pltpu.VMEM((shards, 8, blk), I32),
            pltpu.SMEM((lines, blk), I32),
            pltpu.SemaphoreType.DMA,
            pltpu.SemaphoreType.DMA((count,)),
        ],
        compiler_params=pltpu.CompilerParams(vmem_limit_bytes=50 * 2**20),
        cost_estimate=cost(0.001),
        name="prepare",
    )(*gathered, hidden_grad)

    back_early, tile_sums = pl.pallas_call(
        functools.partial(first_kernel, n_tensor),
        out_shape=(shape((count * cut + lines, blk), BF16), shape((count, blk, blk), F32)),
        in_specs=[vmem] * (3 + n_tensor),
        out_specs=(vmem, vmem),
        scratch_shapes=[
            pltpu.VMEM((count, cut, blk), BF16),
            pltpu.VMEM((2, count, cut, blk), F32),
            pltpu.VMEM((count, cut, blk), BF16),
            pltpu.VMEM((count, cut, blk), F32),
        ],
        compiler_params=spare,
        cost_estimate=cost(0.001),
        name="early_terms",
    )(listed, weights, tokens, hb, *early)

    own, send, back_late = pl.pallas_call(
        functools.partial(second_kernel, n_tensor, cut, cap),
        out_shape=(
            shape((shards, 2, blk, blk), F32),
            shape((shards, 2, blk, blk), BF16),
            shape((count * rest, blk), BF16),
        ),
        in_specs=[vmem] * (4 + n_tensor),
        out_specs=(vmem,) * 3,
        scratch_shapes=[
            pltpu.VMEM((count, rest, blk), BF16),
            pltpu.VMEM((count, rest, blk), BF16),
            pltpu.VMEM((2, count, rest, blk), F32),
            pltpu.VMEM((cap, shards, 2, blk, blk), F32),
            pltpu.VMEM((count, rest, blk), F32),
        ],
        compiler_params=spare,
        cost_estimate=cost(0.001),
        name="late_tiles",
    )(listed, weights, tokens, hb, tile_sums, *late)
    other = lax.ppermute(send, "seq", swap)
    mine, *rounded = pl.pallas_call(
        pair_kernel,
        out_shape=(shape((2, blk, blk), F32),) + (shape((2, blk, blk), BF16),) * (shards - 1),
        in_specs=[vmem, vmem],
        out_specs=(vmem,) * shards,
        compiler_params=spare,
        cost_estimate=cost(0.001),
        name="pair",
    )(own, other)
    others = [
        lax.ppermute(rounded[k - 1], "fsdp", swaps(shards, k)) for k in order
    ]

    def of_all(a):
        if n_tensor == 2:
            return [a, lax.ppermute(a, "tensor", swap)]
        everyone = lax.all_gather(a, "tensor")
        return [everyone[n] for n in range(n_tensor)]

    def scratch(size):
        return [
            pltpu.VMEM((n_tensor, lines, blk), I32),
            pltpu.VMEM((size, width), BF16),
            pltpu.VMEM((size, width) if n_tensor != 2 else (8, 128), F32),
            pltpu.SemaphoreType.DMA,
        ]

    parts = of_all(back_early)
    infos = [part[count * cut :] for part in parts]
    token_grad = pl.pallas_call(
        functools.partial(place_early_kernel, n_tensor, count),
        out_shape=shape((toks, width), BF16),
        in_specs=[vmem] * (2 * n_tensor),
        out_specs=hbm,
        scratch_shapes=scratch(cut),
        compiler_params=spare,
        cost_estimate=cost(0.001),
        name="place_early",
    )(*infos, *parts)
    token_grad = pl.pallas_call(
        functools.partial(place_late_kernel, n_tensor, cut, count),
        out_shape=shape((toks, width), BF16),
        in_specs=[vmem] * (2 * n_tensor) + [hbm],
        out_specs=hbm,
        scratch_shapes=scratch(rest),
        input_output_aliases={2 * n_tensor: 0},
        compiler_params=spare,
        cost_estimate=cost(0.001),
        name="place_late",
    )(*infos, *of_all(back_late), token_grad)
    token_grad, mine = lax.optimization_barrier((token_grad, mine))
    tile_grads = pl.pallas_call(
        sum_kernel,
        out_shape=shape((2, blk, blk), BF16),
        in_specs=[vmem] * shards,
        out_specs=vmem,
        compiler_params=spare,
        cost_estimate=cost(0.001),
        name="sum",
    )(mine, *others)
    return token_grad, tile_grads.reshape(1, 1, 1, 2, blk, blk)


def solution(mesh):
    return jax.shard_map(
        functools.partial(local, dict(mesh.shape)),
        mesh=mesh,
        in_specs=(
            P(("group", "fsdp", "seq"), "tensor"),
            P(("group", "fsdp", "seq"), "tensor"),
            P("fsdp", "tensor", None, None, None, None),
            P("fsdp", "tensor", None, None),
            P("fsdp", "tensor", None),
        ),
        out_specs=(
            P(("group", "fsdp", "seq"), None),
            P(("group", "fsdp"), "tensor", "seq", None, None, None),
        ),
        check_vma=False,
    )
```

```python
import functools

import jax
import jax.numpy as jnp
from jax import lax
from jax.experimental import pallas as pl
from jax.experimental.pallas import tpu as pltpu
from jax.sharding import PartitionSpec as P

F32 = jnp.float32
BF16 = jnp.bfloat16
I32 = jnp.int32
ROW, COL, SLOT, CFIRST, RFIRST = range(5)
INFO_ROWS = 16
ZERO_PARTS = 8


def shift(size, k):
    return [(i, (i + k) % size) for i in range(size)]


def swaps(size, k):
    return [(i, i ^ k) for i in range(size)]


def loop(count, body):
    if count <= 8:
        for i in range(count):
            body(i)
    else:
        lax.fori_loop(0, count, lambda i, c: (body(i), c)[1], 0)


def add_all(count, values, into, at):
    if count <= 8:
        done = [values(i) for i in range(count)]
        for i in range(count):
            into[at(i)] += done[i]
    else:

        def one(i):
            into[at(i)] += values(i)

        loop(count, one)


def find_first(table, src, dst, count):
    def one(i):
        v = table[i, src]

        def step(n, best):
            at = i - 1 - n
            return jnp.where(table[at, src] == v, at, best).astype(I32)

        if isinstance(i, int):
            best = jnp.int32(i)
            for n in range(i):
                best = step(n, best)
        else:
            best = lax.fori_loop(0, i, step, i)
        table[i, dst] = best

    loop(count, one)


def cost(us):
    return pl.CostEstimate(flops=0, bytes_accessed=int(us * 3.69e6), transcendentals=0)


def dot(a, b, dims):
    return lax.dot_general(a, b, (dims, ((), ())), preferred_element_type=F32)


def pack_kernel(cols, keep, count, tiles, packed):
    _, _, cap, _, blk, _ = tiles.shape
    for j in range(cap):
        for m in range(2):
            packed[pl.ds((2 * j + m) * blk, blk), :] = tiles[0, 0, j, m]
    line = lax.broadcasted_iota(I32, (INFO_ROWS, blk), 0)
    lane = lax.broadcasted_iota(I32, (INFO_ROWS, blk), 1)
    info = jnp.zeros((INFO_ROWS, blk), I32)
    for j in range(cap):
        for m in range(2):
            b = keep[0, 0, j, m]
            r = lax.div(b, jnp.int32(cols))
            c = b - r * cols
            r = jnp.where(j < count[0, 0, m], r, -1)
            here = lane == 2 * j + m
            info = jnp.where(here & (line == 0), r, jnp.where(here & (line == 1), c, info))
    packed[pl.ds(2 * cap * blk, INFO_ROWS), :] = info.astype(F32).astype(BF16)


def prepare_kernel(shards, cap, *refs):
    packed, refs = refs[:shards], refs[shards:]
    hidden, listed, weights, hb, out, info, zeros, table, tsem, hsem, zsem = refs
    zeros[...] = jnp.zeros_like(zeros)
    high = zeros.shape[0]
    clear = [
        pltpu.make_async_copy(zeros, out.at[pl.ds(n * high, high), :], zsem.at[n])
        for n in range(ZERO_PARTS)
    ]
    blk = weights.shape[-1]
    base = 2 * cap * blk
    count = hb.shape[0]
    live = count // 2
    for k in range(shards):
        info[k] = packed[k][pl.ds(base, INFO_ROWS), :].astype(F32)[:8].astype(I32)
    for m in range(2):
        p = jnp.int32(m * live)
        for k in range(shards):
            for j in range(cap):
                r = info[k, 0, 2 * j + m]
                table[p, ROW] = r
                table[p, COL] = info[k, 1, 2 * j + m]
                table[p, SLOT] = k * cap + j
                p = p + jnp.where(r >= 0, 1, 0).astype(I32)

    def column(i):
        at = pl.multiple_of(table[i, COL] * blk, blk)
        return pltpu.make_async_copy(hidden.at[:, pl.ds(at, blk)], hb.at[i], hsem.at[i])

    loop(count, lambda i: column(i).start())
    for c in clear:
        c.start()
    find_first(table, COL, CFIRST, count)
    find_first(table, ROW, RFIRST, count)
    done = pltpu.make_async_copy(table, listed, tsem)
    done.start()
    for m in range(2):
        p = jnp.int32(m * live)
        for k in range(shards):
            for j in range(cap):
                weights[p] = packed[k][pl.ds((2 * j + m) * blk, blk), :]
                p = p + jnp.where(info[k, 0, 2 * j + m] >= 0, 1, 0).astype(I32)
    loop(count, lambda i: column(i).wait())
    done.wait()
    for c in clear:
        c.wait()


def forward_backward(lo, table, weights, tokens, hb, remote, xs, pre, grads):
    count, size, blk = xs.shape
    live = count // 2
    rows_here = remote[0].shape[1] // blk
    n_tensor = len(remote) + 1
    t = lax.axis_index("tensor")
    pre[...] = jnp.zeros_like(pre)

    def product(i):
        r = table[i, ROW]
        part = lax.rem(lax.div(r, rows_here) - t + n_tensor, n_tensor)
        at = pl.multiple_of(lax.rem(r, rows_here) * blk, blk)
        x = tokens[pl.ds(lo, size), pl.ds(at, blk)]
        for n, ref in enumerate(remote):
            x = jnp.where(part == n + 1, ref[:, pl.ds(at, blk)], x)
        xs[i] = x
        return dot(x, weights[i], ((1,), (0,)))

    add_all(count, product, pre, lambda i: (i // live, table[i, CFIRST]))

    def backward(i):
        m = i // live
        f = table[i, CFIRST]
        gate = pre[0, f]
        h = hb[i, pl.ds(lo, size), :].astype(F32)
        sig = 1.0 / (1.0 + jnp.exp(-gate))

        def of_gate():
            return h * pre[1, f] * sig * (1.0 + gate * (1.0 - sig))

        def of_up():
            return h * gate * sig

        if isinstance(m, int):
            grad = of_up() if m else of_gate()
        else:
            grad = jnp.where(m == 0, of_gate(), of_up())
        grads[i] = grad.astype(BF16)

    loop(count, backward)


def back_terms(table, weights, grads, acc, back):
    count, size, _ = acc.shape
    acc[...] = jnp.zeros_like(acc)

    def put(i):
        back[pl.ds(pl.multiple_of(i * size, size), size), :] = acc[i].astype(BF16)

    add_all(
        count,
        lambda i: dot(grads[i], weights[i], ((1,), (1,))),
        acc,
        lambda i: table[i, RFIRST],
    )
    loop(count, put)


def first_kernel(n_tensor, table, weights, tokens, hb, *refs):
    remote, refs = refs[: n_tensor - 1], refs[n_tensor - 1 :]
    back, tile_sums, xs, pre, grads, acc = refs
    forward_backward(0, table, weights, tokens, hb, remote, xs, pre, grads)

    def tile(i):
        tile_sums[i] = dot(xs[i], grads[i], ((0,), (0,)))

    count, size, blk = xs.shape
    loop(count, tile)
    back_terms(table, weights, grads, acc, back)
    lines = back.shape[0] - count * size
    line = lax.broadcasted_iota(I32, (lines, blk), 0)
    rows = jnp.zeros((lines, blk), I32)
    for i in range(count):
        rows = jnp.where(line == i, table[i, ROW], rows)
    back[pl.ds(count * size, lines), :] = rows.astype(F32).astype(BF16)


def second_kernel(n_tensor, lo, cap, table, weights, tokens, hb, tile_sums, *refs):
    remote, refs = refs[: n_tensor - 1], refs[n_tensor - 1 :]
    own, send, back, grads, xs, pre, both, acc = refs
    both[...] = jnp.zeros_like(both)
    forward_backward(lo, table, weights, tokens, hb, remote, xs, pre, grads)
    s = lax.axis_index("seq")
    live = xs.shape[0] // 2

    def put(i, value):
        slot = table[i, SLOT]
        both[lax.rem(slot + s, cap), lax.div(slot, cap), i // live] = value

    def tile(i):
        put(i, tile_sums[i] + dot(xs[i], grads[i], ((0,), (0,))))

    loop(xs.shape[0], tile)
    own[...] = both[0]
    send[...] = both[1].astype(send.dtype)
    back_terms(table, weights, grads, acc, back)


def pair_kernel(own, other, *sums):
    for k, total in enumerate(sums):
        total[...] = (own[k] + other[k].astype(F32)).astype(total.dtype)


def place_kernel(n_tensor, count, lo, *refs):
    infos, refs = refs[:n_tensor], refs[n_tensor:]
    parts, refs = refs[:n_tensor], refs[n_tensor:]
    _, out, rows, total, wide, sems = refs
    for n, info in enumerate(infos):
        rows[n] = info[...].astype(F32).astype(I32)
    if n_tensor != 2:
        wide[...] = jnp.zeros_like(wide)
        size, blk = wide.shape[0], parts[0].shape[1]
        for n, part in enumerate(parts):

            def add(i):
                at = pl.ds(pl.multiple_of(rows[n, i, 0] * blk, blk), blk)
                wide[:, at] += part[pl.ds(pl.multiple_of(i * size, size), size), :].astype(F32)

            loop(count, add)
        total[...] = wide[...].astype(BF16)
        copy = pltpu.make_async_copy(total, out.at[pl.ds(lo, size), :], sems.at[0])
        copy.start()
        copy.wait()
        return
    _, size, blk = total.shape
    where = [rows[n, i, 0] for n in range(2) for i in range(count)]
    first = []
    for e, r in enumerate(where):
        f = jnp.int32(e)
        for before in range(e - 1, -1, -1):
            f = jnp.where(where[before] == r, before, f).astype(I32)
        first.append(f)
    for i in range(count):
        total[i] = parts[0][pl.ds(i * size, size), :]
    for i in range(count):
        f = first[count + i]
        term = parts[1][pl.ds(i * size, size), :].astype(F32)
        so_far = jnp.where(f == count + i, 0.0, total[f].astype(F32))
        total[f] = (so_far + term).astype(BF16)

    def copy(e):
        at = pl.ds(pl.multiple_of(where[e] * blk, blk), blk)
        return pltpu.make_async_copy(total.at[e], out.at[pl.ds(lo, size), at], sems.at[e])

    for act in ("start", "wait"):
        for e in range(2 * count):

            @pl.when(first[e] == e)
            def _():
                getattr(copy(e), act)()


def sum_kernel(mine, *refs):
    *others, tile_grads = refs
    total = mine[...]
    for other in others:
        total = total + other[...].astype(F32)
    tile_grads[...] = total.astype(BF16)


def local(sizes, tokens, hidden_grad, tile_blocks, tile_keep, tile_count):
    shards, n_tensor = sizes["fsdp"], sizes["tensor"]
    blk = tile_blocks.shape[-1]
    cap = tile_blocks.shape[2]
    toks = tokens.shape[0]
    width = tokens.shape[1] * n_tensor
    cols = hidden_grad.shape[1] // blk
    count = shards * cap
    cut = toks * 13 // 16 // 16 * 16
    rest = toks - cut
    lines = (count // 16 + 1) * 16
    vmem = pl.BlockSpec(memory_space=pltpu.VMEM)
    smem = pl.BlockSpec(memory_space=pltpu.SMEM)
    hbm = pl.BlockSpec(memory_space=pltpu.HBM)
    spare = pltpu.CompilerParams(vmem_limit_bytes=(16 if count <= 8 else 40) * 2**20)
    swap = shift(2, 1)
    order = [3,1,2] if shards == 4 else list(range(1, shards))

    def shape(dims, kind):
        return jax.ShapeDtypeStruct(dims, kind)

    def to_partners(a):
        return [
            lax.ppermute(a, "tensor", shift(n_tensor, n_tensor - k)) for k in range(1, n_tensor)
        ]

    early = to_partners(tokens[:cut])
    packed = pl.pallas_call(
        functools.partial(pack_kernel, cols),
        out_shape=shape((2 * cap * blk + INFO_ROWS, blk), BF16),
        in_specs=[smem, smem, vmem],
        out_specs=vmem,
        compiler_params=spare,
        cost_estimate=cost(0.001),
        name="pack",
    )(tile_keep, tile_count, tile_blocks)
    late = to_partners(tokens[cut:])
    gathered = [packed] + [
        lax.ppermute(packed, "fsdp", swaps(shards, k)) for k in range(1, shards)
    ]

    listed, weights, hb, token_grad = pl.pallas_call(
        functools.partial(prepare_kernel, shards, cap),
        out_shape=(
            shape((lines, blk), I32),
            shape((count + 1, blk, blk), BF16),
            shape((count, toks, blk), BF16),
            shape((toks, width), BF16),
        ),
        in_specs=[vmem] * shards + [hbm],
        out_specs=(vmem, vmem, vmem, hbm),
        scratch_shapes=[
            pltpu.VMEM((shards, 8, blk), I32),
            pltpu.VMEM((toks // ZERO_PARTS, width), BF16),
            pltpu.SMEM((lines, blk), I32),
            pltpu.SemaphoreType.DMA,
            pltpu.SemaphoreType.DMA((count,)),
            pltpu.SemaphoreType.DMA((ZERO_PARTS,)),
        ],
        compiler_params=pltpu.CompilerParams(vmem_limit_bytes=50 * 2**20),
        cost_estimate=cost(0.001),
        name="prepare",
    )(*gathered, hidden_grad)

    back_early, tile_sums = pl.pallas_call(
        functools.partial(first_kernel, n_tensor),
        out_shape=(shape((count * cut + lines, blk), BF16), shape((count, blk, blk), F32)),
        in_specs=[vmem] * (3 + n_tensor),
        out_specs=(vmem, vmem),
        scratch_shapes=[
            pltpu.VMEM((count, cut, blk), BF16),
            pltpu.VMEM((2, count, cut, blk), F32),
            pltpu.VMEM((count, cut, blk), BF16),
            pltpu.VMEM((count, cut, blk), F32),
        ],
        compiler_params=spare,
        cost_estimate=cost(0.001),
        name="early_terms",
    )(listed, weights, tokens, hb, *early)

    own, send, back_late = pl.pallas_call(
        functools.partial(second_kernel, n_tensor, cut, cap),
        out_shape=(
            shape((shards, 2, blk, blk), F32),
            shape((shards, 2, blk, blk), BF16),
            shape((count * rest, blk), BF16),
        ),
        in_specs=[vmem] * (4 + n_tensor),
        out_specs=(vmem,) * 3,
        scratch_shapes=[
            pltpu.VMEM((count, rest, blk), BF16),
            pltpu.VMEM((count, rest, blk), BF16),
            pltpu.VMEM((2, count, rest, blk), F32),
            pltpu.VMEM((cap, shards, 2, blk, blk), F32),
            pltpu.VMEM((count, rest, blk), F32),
        ],
        compiler_params=spare,
        cost_estimate=cost(0.001),
        name="late_tiles",
    )(listed, weights, tokens, hb, tile_sums, *late)
    other = lax.ppermute(send, "seq", swap)
    mine, *rounded = pl.pallas_call(
        pair_kernel,
        out_shape=(shape((2, blk, blk), F32),) + (shape((2, blk, blk), BF16),) * (shards - 1),
        in_specs=[vmem, vmem],
        out_specs=(vmem,) * shards,
        compiler_params=spare,
        cost_estimate=cost(0.001),
        name="pair",
    )(own, other)
    others = [
        lax.ppermute(rounded[k - 1], "fsdp", swaps(shards, k)) for k in order
    ]

    def of_all(a):
        if n_tensor == 2:
            return [a, lax.ppermute(a, "tensor", swap)]
        everyone = lax.all_gather(a, "tensor")
        return [everyone[n] for n in range(n_tensor)]

    def scratch(size):
        if n_tensor == 2:
            total, wide = (2 * count, size, blk), (8, 128)
        else:
            total, wide = (size, width), (size, width)
        return [
            pltpu.VMEM((n_tensor, lines, blk), I32),
            pltpu.VMEM(total, BF16),
            pltpu.VMEM(wide, F32),
            pltpu.SemaphoreType.DMA((2 * count,)),
        ]

    parts = of_all(back_early)
    infos = [part[count * cut :] for part in parts]
    for name, lo, size, chunk in (
        ("place_early", 0, cut, parts),
        ("place_late", cut, rest, of_all(back_late)),
    ):
        token_grad = pl.pallas_call(
            functools.partial(place_kernel, n_tensor, count, lo),
            out_shape=shape((toks, width), BF16),
            in_specs=[vmem] * (2 * n_tensor) + [hbm],
            out_specs=hbm,
            scratch_shapes=scratch(size),
            input_output_aliases={2 * n_tensor: 0},
            compiler_params=spare,
            cost_estimate=cost(0.001),
            name=name,
        )(*infos, *chunk, token_grad)
    token_grad, mine = lax.optimization_barrier((token_grad, mine))
    tile_grads = pl.pallas_call(
        sum_kernel,
        out_shape=shape((2, blk, blk), BF16),
        in_specs=[vmem] * shards,
        out_specs=vmem,
        compiler_params=spare,
        cost_estimate=cost(0.001),
        name="sum",
    )(mine, *others)
    return token_grad, tile_grads.reshape(1, 1, 1, 2, blk, blk)


def solution(mesh):
    return jax.shard_map(
        functools.partial(local, dict(mesh.shape)),
        mesh=mesh,
        in_specs=(
            P(("group", "fsdp", "seq"), "tensor"),
            P(("group", "fsdp", "seq"), "tensor"),
            P("fsdp", "tensor", None, None, None, None),
            P("fsdp", "tensor", None, None),
            P("fsdp", "tensor", None),
        ),
        out_specs=(
            P(("group", "fsdp", "seq"), None),
            P(("group", "fsdp"), "tensor", "seq", None, None, None),
        ),
        check_vma=False,
    )
```

```python
import functools

import jax
import jax.numpy as jnp
from jax import lax
from jax.experimental import pallas as pl
from jax.experimental.pallas import tpu as pltpu
from jax.sharding import PartitionSpec as P

F32 = jnp.float32
BF16 = jnp.bfloat16
I32 = jnp.int32
ROW, COL, SLOT, CFIRST, RFIRST = range(5)
INFO_ROWS = 16


def shift(size, k):
    return [(i, (i + k) % size) for i in range(size)]


def swaps(size, k):
    return [(i, i ^ k) for i in range(size)]


def loop(count, body):
    if count <= 8:
        for i in range(count):
            body(i)
    else:
        lax.fori_loop(0, count, lambda i, c: (body(i), c)[1], 0)


def add_all(count, values, into, at):
    if count <= 8:
        done = [values(i) for i in range(count)]
        for i in range(count):
            into[at(i)] += done[i]
    else:

        def one(i):
            into[at(i)] += values(i)

        loop(count, one)


def find_first(table, src, dst, count):
    def one(i):
        v = table[i, src]

        def step(n, best):
            at = i - 1 - n
            return jnp.where(table[at, src] == v, at, best).astype(I32)

        if isinstance(i, int):
            best = jnp.int32(i)
            for n in range(i):
                best = step(n, best)
        else:
            best = lax.fori_loop(0, i, step, i)
        table[i, dst] = best

    loop(count, one)


def cost(us):
    return pl.CostEstimate(flops=0, bytes_accessed=int(us * 3.69e6), transcendentals=0)


def dot(a, b, dims):
    return lax.dot_general(a, b, (dims, ((), ())), preferred_element_type=F32)


def pack_kernel(cols, keep, count, tiles, packed):
    _, _, cap, _, blk, _ = tiles.shape
    for j in range(cap):
        for m in range(2):
            packed[pl.ds((2 * j + m) * blk, blk), :] = tiles[0, 0, j, m]
    line = lax.broadcasted_iota(I32, (INFO_ROWS, blk), 0)
    lane = lax.broadcasted_iota(I32, (INFO_ROWS, blk), 1)
    info = jnp.zeros((INFO_ROWS, blk), I32)
    for j in range(cap):
        for m in range(2):
            b = keep[0, 0, j, m]
            r = lax.div(b, jnp.int32(cols))
            c = b - r * cols
            r = jnp.where(j < count[0, 0, m], r, -1)
            here = lane == 2 * j + m
            info = jnp.where(here & (line == 0), r, jnp.where(here & (line == 1), c, info))
    packed[pl.ds(2 * cap * blk, INFO_ROWS), :] = info.astype(F32).astype(BF16)


def prepare_kernel(shards, cap, *refs):
    packed, refs = refs[:shards], refs[shards:]
    hidden, listed, weights, hb, info, table, tsem, hsem = refs
    blk = weights.shape[-1]
    base = 2 * cap * blk
    count = hb.shape[0]
    live = count // 2
    for k in range(shards):
        info[k] = packed[k][pl.ds(base, INFO_ROWS), :].astype(F32)[:8].astype(I32)
    for m in range(2):
        p = jnp.int32(m * live)
        for k in range(shards):
            for j in range(cap):
                r = info[k, 0, 2 * j + m]
                table[p, ROW] = r
                table[p, COL] = info[k, 1, 2 * j + m]
                table[p, SLOT] = k * cap + j
                p = p + jnp.where(r >= 0, 1, 0).astype(I32)

    def column(i):
        at = pl.multiple_of(table[i, COL] * blk, blk)
        return pltpu.make_async_copy(hidden.at[:, pl.ds(at, blk)], hb.at[i], hsem.at[i])

    loop(count, lambda i: column(i).start())
    find_first(table, COL, CFIRST, count)
    find_first(table, ROW, RFIRST, count)
    done = pltpu.make_async_copy(table, listed, tsem)
    done.start()
    for m in range(2):
        p = jnp.int32(m * live)
        for k in range(shards):
            for j in range(cap):
                weights[p] = packed[k][pl.ds((2 * j + m) * blk, blk), :]
                p = p + jnp.where(info[k, 0, 2 * j + m] >= 0, 1, 0).astype(I32)
    loop(count, lambda i: column(i).wait())
    done.wait()


def forward_backward(lo, table, weights, tokens, hb, remote, xs, pre, grads):
    count, size, blk = xs.shape
    live = count // 2
    rows_here = remote[0].shape[1] // blk
    n_tensor = len(remote) + 1
    t = lax.axis_index("tensor")
    pre[...] = jnp.zeros_like(pre)

    def product(i):
        r = table[i, ROW]
        part = lax.rem(lax.div(r, rows_here) - t + n_tensor, n_tensor)
        at = pl.multiple_of(lax.rem(r, rows_here) * blk, blk)
        x = tokens[pl.ds(lo, size), pl.ds(at, blk)]
        for n, ref in enumerate(remote):
            x = jnp.where(part == n + 1, ref[:, pl.ds(at, blk)], x)
        xs[i] = x
        return dot(x, weights[i], ((1,), (0,)))

    add_all(count, product, pre, lambda i: (i // live, table[i, CFIRST]))

    def backward(i):
        m = i // live
        f = table[i, CFIRST]
        gate = pre[0, f]
        h = hb[i, pl.ds(lo, size), :].astype(F32)
        sig = 1.0 / (1.0 + jnp.exp(-gate))

        def of_gate():
            return h * pre[1, f] * sig * (1.0 + gate * (1.0 - sig))

        def of_up():
            return h * gate * sig

        if isinstance(m, int):
            grad = of_up() if m else of_gate()
        else:
            grad = jnp.where(m == 0, of_gate(), of_up())
        grads[i] = grad.astype(BF16)

    loop(count, backward)


def back_terms(table, weights, grads, acc, back):
    count, size, _ = acc.shape
    acc[...] = jnp.zeros_like(acc)

    def put(i):
        back[pl.ds(pl.multiple_of(i * size, size), size), :] = acc[i].astype(BF16)

    add_all(
        count,
        lambda i: dot(grads[i], weights[i], ((1,), (1,))),
        acc,
        lambda i: table[i, RFIRST],
    )
    loop(count, put)


def first_kernel(n_tensor, table, weights, tokens, hb, *refs):
    remote, refs = refs[: n_tensor - 1], refs[n_tensor - 1 :]
    back, tile_sums, xs, pre, grads, acc = refs
    forward_backward(0, table, weights, tokens, hb, remote, xs, pre, grads)

    def tile(i):
        tile_sums[i] = dot(xs[i], grads[i], ((0,), (0,)))

    count, size, blk = xs.shape
    loop(count, tile)
    back_terms(table, weights, grads, acc, back)
    lines = back.shape[0] - count * size
    line = lax.broadcasted_iota(I32, (lines, blk), 0)
    rows = jnp.zeros((lines, blk), I32)
    for i in range(count):
        rows = jnp.where(line == i, table[i, ROW], rows)
    back[pl.ds(count * size, lines), :] = rows.astype(F32).astype(BF16)


def second_kernel(n_tensor, lo, cap, table, weights, tokens, hb, tile_sums, *refs):
    remote, refs = refs[: n_tensor - 1], refs[n_tensor - 1 :]
    own, send, back, grads, xs, pre, both, acc = refs
    both[...] = jnp.zeros_like(both)
    forward_backward(lo, table, weights, tokens, hb, remote, xs, pre, grads)
    s = lax.axis_index("seq")
    live = xs.shape[0] // 2

    def put(i, value):
        slot = table[i, SLOT]
        both[lax.rem(slot + s, cap), lax.div(slot, cap), i // live] = value

    def tile(i):
        put(i, tile_sums[i] + dot(xs[i], grads[i], ((0,), (0,))))

    loop(xs.shape[0], tile)
    own[...] = both[0]
    send[...] = both[1].astype(send.dtype)
    back_terms(table, weights, grads, acc, back)


def pair_kernel(own, other, *sums):
    for k, total in enumerate(sums):
        total[...] = (own[k] + other[k].astype(F32)).astype(total.dtype)


def place_chunk(n_tensor, count, lo, refs, meanwhile=None):
    infos, refs = refs[:n_tensor], refs[n_tensor:]
    parts, refs = refs[:n_tensor], refs[n_tensor:]
    out, rows, block, wide, sem = refs
    size = block.shape[0]
    blk = parts[0].shape[1]
    for n, info in enumerate(infos):
        rows[n] = info[...].astype(F32).astype(I32)
    total = block if n_tensor == 2 else wide
    total[...] = jnp.zeros_like(total)
    if meanwhile is not None:
        meanwhile()
    for n, part in enumerate(parts):

        def add(i):
            at = pl.ds(pl.multiple_of(rows[n, i, 0] * blk, blk), blk)
            term = part[pl.ds(pl.multiple_of(i * size, size), size), :].astype(F32)
            total[:, at] = (total[:, at].astype(F32) + term).astype(total.dtype)

        loop(count, add)
    if n_tensor != 2:
        block[...] = wide[...].astype(BF16)
    copy = pltpu.make_async_copy(block, out.at[pl.ds(lo, size), :], sem)
    copy.start()
    copy.wait()


def place_early_kernel(n_tensor, count, *refs):
    place_chunk(n_tensor, count, 0, refs)


def place_late_kernel(n_tensor, lo, count, *refs):
    first, (_, *rest) = refs[: 2 * n_tensor], refs[2 * n_tensor :]
    place_chunk(n_tensor, count, lo, (*first, *rest))


def sum_kernel(mine, *refs):
    *others, tile_grads = refs
    total = mine[...]
    for other in others:
        total = total + other[...].astype(F32)
    tile_grads[...] = total.astype(BF16)


def local(sizes, tokens, hidden_grad, tile_blocks, tile_keep, tile_count):
    shards, n_tensor = sizes["fsdp"], sizes["tensor"]
    blk = tile_blocks.shape[-1]
    cap = tile_blocks.shape[2]
    toks = tokens.shape[0]
    width = tokens.shape[1] * n_tensor
    cols = hidden_grad.shape[1] // blk
    count = shards * cap
    cut = toks * 13 // 16 // 16 * 16
    rest = toks - cut
    lines = (count // 16 + 1) * 16
    vmem = pl.BlockSpec(memory_space=pltpu.VMEM)
    smem = pl.BlockSpec(memory_space=pltpu.SMEM)
    hbm = pl.BlockSpec(memory_space=pltpu.HBM)
    spare = pltpu.CompilerParams(vmem_limit_bytes=(16 if count <= 8 else 40) * 2**20)
    swap = shift(2, 1)
    order = [shards // 2] + [k for k in range(shards - 1, 0, -1) if k != shards // 2]

    def shape(dims, kind):
        return jax.ShapeDtypeStruct(dims, kind)

    def to_partners(a):
        return [
            lax.ppermute(a, "tensor", shift(n_tensor, n_tensor - k)) for k in range(1, n_tensor)
        ]

    early = to_partners(tokens[:cut])
    packed = pl.pallas_call(
        functools.partial(pack_kernel, cols),
        out_shape=shape((2 * cap * blk + INFO_ROWS, blk), BF16),
        in_specs=[smem, smem, vmem],
        out_specs=vmem,
        compiler_params=spare,
        cost_estimate=cost(0.001),
        name="pack",
    )(tile_keep, tile_count, tile_blocks)
    late = to_partners(tokens[cut:])
    gathered = [packed] + [
        lax.ppermute(packed, "fsdp", swaps(shards, k)) for k in range(1, shards)
    ]

    listed, weights, hb = pl.pallas_call(
        functools.partial(prepare_kernel, shards, cap),
        out_shape=(
            shape((lines, blk), I32),
            shape((count + 1, blk, blk), BF16),
            shape((count, toks, blk), BF16),
        ),
        in_specs=[vmem] * shards + [hbm],
        out_specs=(vmem, vmem, vmem),
        scratch_shapes=[
            pltpu.VMEM((shards, 8, blk), I32),
            pltpu.SMEM((lines, blk), I32),
            pltpu.SemaphoreType.DMA,
            pltpu.SemaphoreType.DMA((count,)),
        ],
        compiler_params=pltpu.CompilerParams(vmem_limit_bytes=50 * 2**20),
        cost_estimate=cost(0.001),
        name="prepare",
    )(*gathered, hidden_grad)

    back_early, tile_sums = pl.pallas_call(
        functools.partial(first_kernel, n_tensor),
        out_shape=(shape((count * cut + lines, blk), BF16), shape((count, blk, blk), F32)),
        in_specs=[vmem] * (3 + n_tensor),
        out_specs=(vmem, vmem),
        scratch_shapes=[
            pltpu.VMEM((count, cut, blk), BF16),
            pltpu.VMEM((2, count, cut, blk), F32),
            pltpu.VMEM((count, cut, blk), BF16),
            pltpu.VMEM((count, cut, blk), F32),
        ],
        compiler_params=spare,
        cost_estimate=cost(0.001),
        name="early_terms",
    )(listed, weights, tokens, hb, *early)

    own, send, back_late = pl.pallas_call(
        functools.partial(second_kernel, n_tensor, cut, cap),
        out_shape=(
            shape((shards, 2, blk, blk), F32),
            shape((shards, 2, blk, blk), BF16),
            shape((count * rest, blk), BF16),
        ),
        in_specs=[vmem] * (4 + n_tensor),
        out_specs=(vmem,) * 3,
        scratch_shapes=[
            pltpu.VMEM((count, rest, blk), BF16),
            pltpu.VMEM((count, rest, blk), BF16),
            pltpu.VMEM((2, count, rest, blk), F32),
            pltpu.VMEM((cap, shards, 2, blk, blk), F32),
            pltpu.VMEM((count, rest, blk), F32),
        ],
        compiler_params=spare,
        cost_estimate=cost(0.001),
        name="late_tiles",
    )(listed, weights, tokens, hb, tile_sums, *late)
    other = lax.ppermute(send, "seq", swap)
    mine, *rounded = pl.pallas_call(
        pair_kernel,
        out_shape=(shape((2, blk, blk), F32),) + (shape((2, blk, blk), BF16),) * (shards - 1),
        in_specs=[vmem, vmem],
        out_specs=(vmem,) * shards,
        compiler_params=spare,
        cost_estimate=cost(0.001),
        name="pair",
    )(own, other)
    others = [
        lax.ppermute(rounded[k - 1], "fsdp", swaps(shards, k)) for k in order
    ]

    def of_all(a):
        if n_tensor == 2:
            return [a, lax.ppermute(a, "tensor", swap)]
        everyone = lax.all_gather(a, "tensor")
        return [everyone[n] for n in range(n_tensor)]

    def scratch(size):
        return [
            pltpu.VMEM((n_tensor, lines, blk), I32),
            pltpu.VMEM((size, width), BF16),
            pltpu.VMEM((size, width) if n_tensor != 2 else (8, 128), F32),
            pltpu.SemaphoreType.DMA,
        ]

    parts = of_all(back_early)
    infos = [part[count * cut :] for part in parts]
    token_grad = pl.pallas_call(
        functools.partial(place_early_kernel, n_tensor, count),
        out_shape=shape((toks, width), BF16),
        in_specs=[vmem] * (2 * n_tensor),
        out_specs=hbm,
        scratch_shapes=scratch(cut),
        compiler_params=spare,
        cost_estimate=cost(0.001),
        name="place_early",
    )(*infos, *parts)
    token_grad = pl.pallas_call(
        functools.partial(place_late_kernel, n_tensor, cut, count),
        out_shape=shape((toks, width), BF16),
        in_specs=[vmem] * (2 * n_tensor) + [hbm],
        out_specs=hbm,
        scratch_shapes=scratch(rest),
        input_output_aliases={2 * n_tensor: 0},
        compiler_params=spare,
        cost_estimate=cost(0.001),
        name="place_late",
    )(*infos, *of_all(back_late), token_grad)
    token_grad, mine = lax.optimization_barrier((token_grad, mine))
    tile_grads = pl.pallas_call(
        sum_kernel,
        out_shape=shape((2, blk, blk), BF16),
        in_specs=[vmem] * shards,
        out_specs=vmem,
        compiler_params=spare,
        cost_estimate=cost(0.001),
        name="sum",
    )(mine, *others)
    return token_grad, tile_grads.reshape(1, 1, 1, 2, blk, blk)


def solution(mesh):
    return jax.shard_map(
        functools.partial(local, dict(mesh.shape)),
        mesh=mesh,
        in_specs=(
            P(("group", "fsdp", "seq"), "tensor"),
            P(("group", "fsdp", "seq"), "tensor"),
            P("fsdp", "tensor", None, None, None, None),
            P("fsdp", "tensor", None, None),
            P("fsdp", "tensor", None),
        ),
        out_specs=(
            P(("group", "fsdp", "seq"), None),
            P(("group", "fsdp"), "tensor", "seq", None, None, None),
        ),
        check_vma=False,
    )
```
